256 devices in a mesh: path: 64 (over z, x, core), shard: 4 (over y).
Axes of the slice: x: 4, y: 4, z: 8, core: 2. Of those that a mesh axis runs over, the one named last changes fastest.
Arguments:
- pseudo_grad: bfloat16 [256, 16, 64, 1024], P('path', None, 'shard')
- kept_index: int32 [256, 16, 16, 16], P('path'), may hold values from 0 to 63, as said below
- usage: int32 [256, 16], replicated, may hold values from 0 to 15
- module_params: bfloat16 [256, 64, 1024], P('path', 'shard'), may hold values from -6 to 6
- momentum: float32 [256, 64, 1024], P('path', 'shard'), may hold values from -4 to 4
Outputs:
- new_params: bfloat16 [256, 64, 1024], P('path', 'shard')
- new_momentum: float32 [256, 64, 1024], P('path', 'shard')
- path_params: bfloat16 [256, 16, 64, 1024], P('path', None, 'shard')
The draws below stay inside these ranges and needn't reach their ends.
Inputs may be any that keep to these rules, and one draw needn't show every extreme that they name: `kept_index`: the 16 indices of one block are distinct.
All inputs are finite; a program needn't handle non-finite values.
Results may differ from the reference program's by a relative error of at most 0.0049.
Values may be sent and summed in bfloat16 or wider, within the bound.
No kernel may reach another device: no remote copies, remote signals or barrier semaphores. Data moves between devices by JAX's collectives and lax.ppermute only.
A program may use at most 128 MiB of HBM per device.

```python
import math
import jax
import jax.numpy as jnp
import numpy as np
from jax import lax

D = 1024
CH = 64
KEEP = 16
LEVELS = 16
OPTIONS = 16
ROWS = 64
PATHS = 256
MODULES = 256


def draw_pseudo_grad(key, part):
    key = jax.random.fold_in(key, 5)
    first, second, third = jax.random.split(key, 3)
    shape = (PATHS, LEVELS, ROWS, D)
    base = jax.random.normal(first, shape, jnp.float32)
    rising = jnp.arange(ROWS, dtype=jnp.float32)[:, None] / ROWS
    row_part = jax.random.uniform(second, (PATHS, LEVELS, ROWS, 1), jnp.float32, -0.5, 0.5)
    column_part = jax.random.uniform(third, (1, 1, 1, D), jnp.float32, -0.5, 0.5)
    scaling = jnp.exp(math.log(3.0) * rising + math.log(10.0) * (row_part + column_part))
    return (0.5 * base * scaling).astype(jnp.bfloat16)


def draw_kept_index(key, part):
    key = jax.random.fold_in(key, 11)
    random_bits = jax.random.randint(key, (PATHS, LEVELS, D // CH, CH), 0, 1 << 20)
    scores = random_bits * CH + jnp.arange(CH, dtype=jnp.int32)
    ranking = jnp.argsort(scores, axis=-1)
    return ranking[..., :KEEP].astype(jnp.int32)


def touch_ends(values, rng, least, top_value):
    dims = values.shape
    place = [jax.random.randint(jax.random.fold_in(rng, axis), (), 0, dims[axis]) for axis in range(len(dims))]
    values = values.at[tuple(place)].set(least)
    longest = dims.index(max(dims))
    place[longest] = (place[longest] + 1) % dims[longest]
    return values.at[tuple(place)].set(top_value)


def level_of(stream_key, extent, shards, smallest, top_value):
    loudness = 1.0
    for dim, shards_of in shards:
        draws = jax.random.uniform(jax.random.fold_in(jax.random.fold_in(stream_key, 6), dim), (shards_of,), jnp.float32, smallest / len(shards), top_value / len(shards))
        loudness = loudness * jnp.repeat(jnp.exp(draws), extent[dim] // shards_of).reshape((-1,) + (1,) * (len(extent) - 1 - dim))
    return loudness


def rank_bounds(number_of, lean):
    weights = [(1 << 20) // math.isqrt(rank ** lean) + 1 for rank in range(1, number_of + 1)]
    scale = 1 + sum(weights) // (1 << 30)
    return np.cumsum(np.array([max(1, weight // scale) for weight in weights]))


def skewed_ids(rng, dims, amount, lean):
    listing = rank_bounds(amount, lean)
    ticket = jax.random.randint(jax.random.fold_in(rng, 1), dims, 0, int(listing[amount - 1]))
    grade = jnp.searchsorted(jnp.asarray(listing, jnp.int32), ticket, side="right")
    return jax.random.permutation(jax.random.fold_in(rng, 2), amount)[grade].astype(jnp.int32)


def bell_draw(stream_key, dims, deviation, limit, shards=(), held_as=jnp.bfloat16):
    values = jax.random.normal(stream_key, dims, jnp.float32) * deviation
    if len(shards) > 0:
        values = level_of(stream_key, dims, shards, -0.22, 0.18) * values
    return jnp.clip(values, min=-limit, max=limit).astype(held_as)


def setup_inputs(seed: int = 0) -> dict:
    seeds = jax.random.split(jax.random.key(seed), 6)
    return {
        "pseudo_grad": draw_pseudo_grad(jax.random.fold_in(seeds[5], 71), 0),
        "kept_index": draw_kept_index(jax.random.fold_in(seeds[5], 71), 0),
        "usage": touch_ends(skewed_ids(seeds[2], (PATHS, LEVELS), OPTIONS, 1), jax.random.fold_in(seeds[2], 3), 0, OPTIONS - 1).astype(jnp.int32),
        "module_params": bell_draw(seeds[3], (MODULES, ROWS, D), 1.0, 6.0, ((0, 64), (1, 4))),
        "momentum": bell_draw(seeds[4], (MODULES, ROWS, D), 0.5, 4.0, ((0, 64), (1, 4)), jnp.float32),
    }


def dct_table(length):
    frequency = lax.broadcasted_iota(jnp.int32, (length, length), 0).astype(jnp.float32)
    position = lax.broadcasted_iota(jnp.int32, (length, length), 1).astype(jnp.float32)
    normalizer = jnp.where(frequency == 0.0, math.sqrt(1.0 / length), math.sqrt(2.0 / length))
    return normalizer * jnp.cos(math.pi * (2.0 * position + 1.0) * frequency / (2.0 * length))

def reference(pseudo_grad, kept_index, usage, module_params, momentum):
    cosine = dct_table(CH)
    stretch_count = D // CH
    modules = LEVELS * OPTIONS
    level_ids = jnp.arange(LEVELS, dtype=jnp.int32)

    def per_path(totals, inputs):
        gradient, kept, usage_row = inputs
        blocks = gradient.astype(jnp.float32).reshape(LEVELS, ROWS, stretch_count, CH)
        spectrum = jnp.einsum('lrcn,kn->lrck', blocks, cosine, precision=lax.Precision.HIGHEST)
        picked = jnp.take_along_axis(spectrum, kept[:, None, :, :], axis=3).astype(jnp.bfloat16)
        selector = (kept[..., None] == jnp.arange(CH, dtype=jnp.int32)).astype(jnp.float32)
        expanded = jnp.einsum('lrck,lckj->lrcj', picked.astype(jnp.float32), selector, precision=lax.Precision.HIGHEST)
        module_ids = level_ids * OPTIONS + usage_row
        totals = totals.at[module_ids].add(expanded.reshape(LEVELS, ROWS, D))
        return (totals, None)
    start = jnp.zeros((modules, ROWS, D), jnp.float32)
    summed, _ = lax.scan(per_path, start, (pseudo_grad, kept_index, usage))
    all_ids = level_ids[None, :] * OPTIONS + usage
    counts = lax.optimization_barrier(jnp.sum((all_ids[..., None] == jnp.arange(modules, dtype=jnp.int32)).astype(jnp.float32), axis=(0, 1)))
    average = summed / jnp.maximum(counts, 1.0)[:, None, None]
    delta = jnp.einsum('mrck,kn->mrcn', average.reshape(modules, ROWS, stretch_count, CH), cosine, precision=lax.Precision.HIGHEST).reshape(modules, ROWS, D)
    squares = lax.optimization_barrier(jnp.mean(delta * delta, axis=(1, 2)))
    factor = jnp.minimum(1.0, 0.3 / jnp.sqrt(squares + 1e-06))
    clipped = delta * factor[:, None, None]
    new_momentum = 0.9 * momentum + clipped
    new_params = (module_params.astype(jnp.float32) - 0.7 * (clipped + 0.9 * new_momentum)).astype(jnp.bfloat16)
    path_params = new_params[all_ids]
    return (new_params, new_momentum, path_params)
```

```python
import functools
import math

import jax
import jax.numpy as jnp
import ml_dtypes
import numpy as np
from jax import lax
from jax.experimental import pallas as pl
from jax.experimental.pallas import tpu as pltpu
from jax.sharding import PartitionSpec as P

CH = 64
KEEP = 16
LEVELS = 16
OPTIONS = 16
ROWS = 16
WIDTH = 1024
PATHS = 256
DEVICES = 64
MINE = 4
QUAD = 4
COLS = WIDTH // QUAD
SENT = 40
F32 = jnp.float32
BF16 = jnp.bfloat16
VMEM_LIMIT = 40 * 1024 * 1024


def dct_tables():
    k = np.arange(CH)[:, None]
    n = np.arange(CH)[None, :]
    scale = np.where(k == 0, math.sqrt(1.0 / CH), math.sqrt(2.0 / CH))
    table = np.kron(np.eye(4), scale * np.cos(math.pi * (2.0 * n + 1.0) * k / (2.0 * CH)))
    high = table.astype(ml_dtypes.bfloat16)
    low = (table - high.astype(np.float64)).astype(ml_dtypes.bfloat16)
    inverse = np.stack([high, low])
    return np.ascontiguousarray(inverse.transpose(0, 2, 1)), inverse


def dot2(values, table_ref):
    return jnp.dot(values, table_ref[0], preferred_element_type=F32) + jnp.dot(
        values, table_ref[1], preferred_element_type=F32
    )


def take_lanes(values, index):
    return jnp.take_along_axis(values, index, axis=1, mode="promise_in_bounds")


def lanes(rows):
    return lax.broadcasted_iota(jnp.int32, (rows, 128), 1)


def base_kernel(q_ref, params_ref, momentum_ref, *out_refs):
    for k in range(QUAD):
        at = pl.ds(pl.multiple_of((q_ref[0] ^ k) * COLS, COLS), COLS)
        for i in range(MINE):
            base = params_ref[i, :, at].astype(F32) - 0.567 * momentum_ref[i, :, at]
            out_refs[k][i * ROWS : (i + 1) * ROWS, :] = base.astype(BF16)


def pick_kernel(grad_ref, kept_ref, table_ref, out_ref, spectrum_ref):
    levels = grad_ref.shape[1]
    grad = grad_ref[...].reshape(MINE * levels * ROWS, WIDTH)
    for q in range(QUAD):
        spectrum_ref[q] = dot2(grad[:, q * COLS : (q + 1) * COLS], table_ref)
    lane = lanes(ROWS)
    shift = ((lane // KEEP) % 2) * CH
    for level in range(levels):
        for q in range(QUAD):
            for pair in range(2):
                index = jnp.broadcast_to(kept_ref[level, q, pair : pair + 1, :], (ROWS, 128)) + shift

                def part(half, tile):
                    start = ((pair * 2 + half) * levels + level) * ROWS
                    rows = spectrum_ref[q, start : start + ROWS, tile * 128 : (tile + 1) * 128]
                    return take_lanes(rows, index)

                first = jnp.where(lane < 32, part(0, 0), part(0, 1))
                second = jnp.where(lane < 96, part(1, 0), part(1, 1))
                picked = jnp.where(lane < 64, first, second)
                out_ref[level * QUAD + q, pair * ROWS : (pair + 1) * ROWS, :] = picked.astype(BF16)
            index_rows = jnp.concatenate(
                [kept_ref[level, q].astype(F32), jnp.zeros((6, 128), F32)], axis=0
            )
            out_ref[level * QUAD + q, 32:40, :] = index_rows.astype(BF16)


def sum_kernel(usage_ref, got_ref, avg_ref, square_ref, *rest):
    peer_refs = rest[:3]
    where_ref = rest[3]
    total_refs = rest[4:8]
    count_ref = rest[8]
    lane = lanes(8)
    block = lane // CH
    k = lane % CH
    for total in total_refs:
        total[...] = jnp.zeros_like(total)
    for o in range(OPTIONS):
        count_ref[o] = 0

    def invert(group, carry):
        at = pl.ds(pl.multiple_of(group * 8, 8), 8)
        index = got_ref[at, 32:40, :].astype(F32)
        for pair in range(2):
            rows = index[:, pair, :].astype(jnp.int32)
            for half in range(2):
                for tile in range(2):
                    base = half * 64 + (tile * 2 + block) * KEEP
                    found = jnp.full((8, 128), -1, jnp.int32)
                    for j in range(KEEP):
                        found = jnp.where(take_lanes(rows, base + j) == k, base + j, found)
                    where_ref[pair * 4 + half * 2 + tile, at, :] = found
        return carry

    lax.fori_loop(0, DEVICES // 8, invert, 0)

    def add(s, carry):
        for pair in range(2):
            values = got_ref[s, pair * ROWS : (pair + 1) * ROWS, :].astype(F32)
            for half in range(2):
                o = usage_ref[s * MINE + pair * 2 + half]
                count_ref[o] += 1
                rows = pl.ds(pl.multiple_of(o * ROWS, ROWS), ROWS)
                total = total_refs[pair * 2 + half]
                for tile in range(2):
                    index = jnp.broadcast_to(
                        where_ref[pair * 4 + half * 2 + tile, pl.ds(s, 1), :], (ROWS, 128)
                    )
                    spread = jnp.where(index >= 0, take_lanes(values, jnp.maximum(index, 0)), 0.0)
                    total[rows, tile * 128 : (tile + 1) * 128] += spread
        return carry

    lax.fori_loop(0, DEVICES, add, 0, unroll=2)

    squares = jnp.zeros((1, 128), F32)
    for o in range(OPTIONS):
        at = slice(o * ROWS, (o + 1) * ROWS)
        summed = (total_refs[0][at, :] + total_refs[1][at, :]) + (
            total_refs[2][at, :] + total_refs[3][at, :]
        )
        average = summed / jnp.maximum(count_ref[o], 1).astype(F32)
        avg_ref[o // MINE, (o % MINE) * ROWS : (o % MINE + 1) * ROWS, :] = average.astype(BF16)
        square = jnp.sum(average * average, axis=(0, 1), keepdims=True)
        squares = jnp.where(lanes(1) == o, square, squares)
    square_ref[...] = jnp.broadcast_to(squares, (8, 128))
    high = squares.astype(BF16).astype(F32)
    middle = (squares - high).astype(BF16).astype(F32)
    low = squares - high - middle
    row = lax.broadcasted_iota(jnp.int32, (16, 128), 0)
    split = jnp.where(row == 0, high, jnp.where(row == 1, middle, jnp.where(row == 2, low, 0.0)))
    for i, peer_ref in enumerate(peer_refs):
        peer_ref[0:64, :] = avg_ref[usage_ref[PATHS] ^ (i + 1)]
        peer_ref[64:80, 0:128] = split.astype(BF16)
        peer_ref[64:80, 128:256] = jnp.zeros((16, 128), BF16)


def clip_factor(square_refs):
    total = (square_refs[0][0:1, :] + square_refs[1][0:1, :]) + (
        square_refs[2][0:1, :] + square_refs[3][0:1, :]
    )
    entries = 4.0 * ROWS * WIDTH
    return jnp.minimum(1.0, 0.3 / jnp.sqrt(total / entries + 1e-06))


def factor_of(factors, module):
    return jnp.sum(jnp.where(lanes(1) == module, factors, 0.0), axis=1, keepdims=True)


def reply_kernel(usage_ref, avg_ref, table_ref, *rest):
    base_refs = rest[:4]
    square_refs = rest[4:8]
    out_ref, fresh_ref = rest[8:]
    step = pl.program_id(0)

    @pl.when(step == 0)
    def _():
        factors = clip_factor(square_refs)
        for k in range(QUAD):
            owner = usage_ref[PATHS] ^ k
            delta = dot2(avg_ref[owner], table_ref)
            for i in range(MINE):
                module = owner * MINE + i
                at = slice(i * ROWS, (i + 1) * ROWS)
                change = (1.33 * factor_of(factors, module)) * delta[at, :]
                fresh = base_refs[k][at, :].astype(F32) - change
                fresh_ref[pl.ds(pl.multiple_of(module * ROWS, ROWS), ROWS), :] = fresh.astype(BF16)

    targets = out_ref.shape[0]
    for d in range(targets):
        for p in range(MINE):
            o = usage_ref[(step * targets + d) * MINE + p]
            out_ref[d, p] = fresh_ref[pl.ds(pl.multiple_of(o * ROWS, ROWS), ROWS), :]


def owner_kernel(usage_ref, avg_ref, table_ref, params_ref, momentum_ref, *rest):
    peer_refs = rest[:3]
    square_refs = rest[3:7]
    new_params_ref, new_momentum_ref = rest[7:]
    q = usage_ref[PATHS]
    factors = clip_factor(square_refs)
    for k in range(QUAD):
        at = pl.ds(pl.multiple_of((q ^ k) * COLS, COLS), COLS)
        average = avg_ref[q] if k == 0 else peer_refs[k - 1][0:64, :]
        delta = dot2(average, table_ref)
        for i in range(MINE):
            clipped = delta[i * ROWS : (i + 1) * ROWS, :] * factor_of(factors, q * MINE + i)
            momentum = 0.9 * momentum_ref[i, :, at] + clipped
            new_momentum_ref[i, :, at] = momentum
            new = params_ref[i, :, at].astype(F32) - 0.7 * (clipped + 0.9 * momentum)
            new_params_ref[i, :, at] = new.astype(BF16)


def place_kernel(got_ref, out_ref):
    for level in range(out_ref.shape[1]):
        for q in range(QUAD):
            for p in range(MINE):
                out_ref[p, level, :, q * COLS : (q + 1) * COLS] = got_ref[level * QUAD + q, p]


def call(kernel, out_shape, **kwargs):
    return pl.pallas_call(
        kernel,
        out_shape=out_shape,
        compiler_params=pltpu.CompilerParams(vmem_limit_bytes=VMEM_LIMIT),
        **kwargs,
    )


def shaped(shape, dtype):
    return jax.ShapeDtypeStruct(shape, dtype)


def swap(values, k):
    return lax.ppermute(values, "path", [(i, i ^ k) for i in range(DEVICES)])


def turn(values, k):
    return lax.ppermute(values, "shard", [(i, (i + k) % 4) for i in range(4)])


def local(pseudo_grad, kept_index, usage, module_params, momentum):
    forward, inverse = dct_tables()
    smem = pl.BlockSpec(memory_space=pltpu.SMEM)
    vmem = pl.BlockSpec(memory_space=pltpu.VMEM)
    device = lax.axis_index("path")
    level, q = device // QUAD, device % QUAD
    used = lax.dynamic_slice_in_dim(usage, level, 1, 1).reshape(PATHS)
    used = jnp.concatenate([used, jnp.full((8,), q, jnp.int32)])

    bases = call(
        base_kernel,
        [shaped((MINE * ROWS, COLS), BF16)] * QUAD,
        in_specs=[smem, vmem, vmem],
        out_specs=[vmem] * QUAD,
    )(jnp.full((1,), q, jnp.int32), module_params, momentum)
    bases = [bases[0]] + [swap(bases[k], k) for k in range(1, QUAD)]

    kept = kept_index.reshape(2, 2, LEVELS, QUAD, 4, KEEP).transpose(2, 3, 0, 1, 4, 5)
    kept = kept.reshape(LEVELS, QUAD, 2, 128)
    span = 4
    outgoing = call(
        pick_kernel,
        shaped((DEVICES, SENT, 128), BF16),
        grid=(LEVELS // span,),
        in_specs=[
            pl.BlockSpec((MINE, span, ROWS, WIDTH), lambda i: (0, i, 0, 0)),
            pl.BlockSpec((span, QUAD, 2, 128), lambda i: (i, 0, 0, 0)),
            pl.BlockSpec((2, COLS, COLS), lambda i: (0, 0, 0)),
        ],
        out_specs=pl.BlockSpec((span * QUAD, SENT, 128), lambda i: (i, 0, 0)),
        scratch_shapes=[pltpu.VMEM((QUAD, MINE * span * ROWS, COLS), F32)],
    )(pseudo_grad, kept, forward)
    got = lax.all_to_all(outgoing, "path", 0, 0, tiled=True)

    average, squares, *pieces = call(
        sum_kernel,
        [shaped((QUAD, MINE * ROWS, COLS), BF16), shaped((8, 128), F32)]
        + [shaped((MINE * ROWS + 16, COLS), BF16)] * 3,
        in_specs=[smem, vmem],
        out_specs=[vmem] * 5,
        scratch_shapes=[pltpu.VMEM((8, DEVICES, 128), jnp.int32)]
        + [pltpu.VMEM((OPTIONS * ROWS, COLS), F32)] * 4
        + [pltpu.SMEM((OPTIONS,), jnp.int32)],
    )(used, got)
    pieces = [swap(piece, k + 1) for k, piece in enumerate(pieces)]
    for piece in pieces:
        squares = squares + jnp.sum(piece[64:67, 0:128].astype(F32), axis=0, keepdims=True)
    all_squares = [squares] + [turn(squares, k) for k in range(1, 4)]

    targets = 8
    replies = call(
        reply_kernel,
        shaped((DEVICES, MINE, ROWS, COLS), BF16),
        grid=(DEVICES // targets,),
        in_specs=[smem] + [vmem] * 10,
        out_specs=pl.BlockSpec((targets, MINE, ROWS, COLS), lambda i: (i, 0, 0, 0)),
        scratch_shapes=[pltpu.VMEM((OPTIONS * ROWS, COLS), BF16)],
    )(used, average, inverse, *bases, *all_squares)
    returned = lax.all_to_all(replies, "path", 0, 0, tiled=True)

    new_params, new_momentum = call(
        owner_kernel,
        [shaped((MINE, ROWS, WIDTH), BF16), shaped((MINE, ROWS, WIDTH), F32)],
        in_specs=[smem] + [vmem] * 11,
        out_specs=[vmem] * 2,
    )(used, average, inverse, module_params, momentum, *pieces, *all_squares)

    span = 2
    path_params = call(
        place_kernel,
        shaped((MINE, LEVELS, ROWS, WIDTH), BF16),
        grid=(LEVELS // span,),
        in_specs=[pl.BlockSpec((span * QUAD, MINE, ROWS, COLS), lambda i: (i, 0, 0, 0))],
        out_specs=pl.BlockSpec((MINE, span, ROWS, WIDTH), lambda i: (0, i, 0, 0)),
    )(returned)
    return (new_params, new_momentum, path_params)


def solution(mesh):
    return jax.shard_map(
        local,
        mesh=mesh,
        in_specs=(
            P("path", None, "shard", None),
            P("path", None, None, None),
            P(),
            P("path", "shard", None),
            P("path", "shard", None),
        ),
        out_specs=(
            P("path", "shard", None),
            P("path", "shard", None),
            P("path", None, "shard", None),
        ),
        check_vma=False,
    )
```

```python
import functools
import math

import jax
import jax.numpy as jnp
import ml_dtypes
import numpy as np
from jax import lax
from jax.experimental import pallas as pl
from jax.experimental.pallas import tpu as pltpu
from jax.sharding import Mesh
from jax.sharding import PartitionSpec as P

CH = 64
KEEP = 16
LEVELS = 16
OPTIONS = 16
ROWS = 16
WIDTH = 1024
PATHS = 256
DEVICES = 64
MINE = 4
QUAD = 4
COLS = WIDTH // QUAD
SENT = 40
F32 = jnp.float32
BF16 = jnp.bfloat16
CHUNKS = 4
VMEM_LIMIT = 40 * 1024 * 1024
STREAM_LIMIT = 56 * 1024 * 1024
PATH = ("level", "quad")
SQUARE_GROUP = ("quad", "shard")


def dct_tables():
    k = np.arange(CH)[:, None]
    n = np.arange(CH)[None, :]
    scale = np.where(k == 0, math.sqrt(1.0 / CH), math.sqrt(2.0 / CH))
    table = np.kron(np.eye(4), scale * np.cos(math.pi * (2.0 * n + 1.0) * k / (2.0 * CH)))
    high = table.astype(ml_dtypes.bfloat16)
    low = (table - high.astype(np.float64)).astype(ml_dtypes.bfloat16)
    inverse = np.stack([high, low])
    return np.ascontiguousarray(inverse.transpose(0, 2, 1)), inverse


def dot2(values, table_ref):
    return jnp.dot(values, table_ref[0], preferred_element_type=F32) + jnp.dot(
        values, table_ref[1], preferred_element_type=F32
    )


def take_lanes(values, index):
    return jnp.take_along_axis(values, index, axis=1, mode="promise_in_bounds")


def lanes(rows):
    return lax.broadcasted_iota(jnp.int32, (rows, 128), 1)


def base_kernel(q_ref, params_ref, momentum_ref, *out_refs):
    for k in range(QUAD):
        at = pl.ds(pl.multiple_of((q_ref[0] ^ k) * COLS, COLS), COLS)
        for i in range(MINE):
            base = params_ref[i, :, at].astype(F32) - 0.567 * momentum_ref[i, :, at]
            out_refs[k][i * ROWS : (i + 1) * ROWS, :] = base


def sort_groups(values):
    lane = lanes(values.shape[0])
    size = 2
    while size <= KEEP:
        distance = size // 2
        while distance >= 1:
            other = take_lanes(values, lane ^ distance)
            upward = (lane & size) == 0 if size < KEEP else lane >= 0
            first = (lane & distance) == 0
            keep_least = first == upward
            values = jnp.where(keep_least, jnp.minimum(values, other), jnp.maximum(values, other))
            distance //= 2
        size *= 2
    return values


def gather_kept(kept_ref, pair):
    rows = LEVELS * 16
    repeat = (lanes(KEEP) % KEEP == lax.broadcasted_iota(jnp.int32, (KEEP, 128), 0)).astype(BF16)
    block = lax.broadcasted_iota(jnp.int32, (rows, 128), 0) % 4
    lane = lanes(rows)
    total = jnp.zeros((rows, 128), F32)
    for half in range(2):
        kept = kept_ref[pair * 2 + half].reshape(rows, KEEP).astype(F32).astype(BF16)
        spread = jnp.dot(kept, repeat, preferred_element_type=F32)
        total = jnp.where(lane // KEEP == half * 4 + block, spread, total)
    row = lax.broadcasted_iota(jnp.int32, (LEVELS * QUAD, rows), 0)
    column = lax.broadcasted_iota(jnp.int32, (LEVELS * QUAD, rows), 1)
    fold = (column // 4 == row).astype(BF16)
    return jnp.dot(fold, total.astype(BF16), preferred_element_type=F32).astype(jnp.int32)


def pick_kernel(
    grad_any,
    kept_any,
    table_any,
    out_any,
    grad_ref,
    kept_ref,
    table_ref,
    spectrum_ref,
    sorted_ref,
    out_ref,
    sems,
):
    kept = pltpu.make_async_copy(kept_any, kept_ref, sems.at[0])
    table = pltpu.make_async_copy(table_any, table_ref, sems.at[1])
    grads = [
        pltpu.make_async_copy(grad_any.at[p], grad_ref.at[p], sems.at[2 + p]) for p in range(MINE)
    ]
    emits = [
        pltpu.make_async_copy(out_ref.at[:, q], out_any.at[:, q], sems.at[2 + MINE + q])
        for q in range(QUAD)
    ]
    for copy in [kept, table] + grads:
        copy.start()
    kept.wait()
    for pair in range(2):
        sorted_ref[pair] = sort_groups(gather_kept(kept_ref, pair))
    lane = lanes(ROWS)
    shift = ((lane // KEEP) % 2) * CH
    for copy in [table] + grads:
        copy.wait()

    for q in range(QUAD):
        grad = grad_ref[:, :, :, q * COLS : (q + 1) * COLS].reshape(MINE * LEVELS * ROWS, COLS)
        spectrum_ref[q] = dot2(grad, table_ref)

        def pick(level, carry):
            for pair in range(2):
                row = sorted_ref[pair, pl.ds(level * QUAD + q, 1), :]
                index = jnp.broadcast_to(row, (ROWS, 128)) + shift

                def part(half, tile):
                    start = ((pair * 2 + half) * LEVELS + level) * ROWS
                    rows = pl.ds(pl.multiple_of(start, ROWS), ROWS)
                    return take_lanes(spectrum_ref[q, rows, tile * 128 : (tile + 1) * 128], index)

                first = jnp.where(lane < 32, part(0, 0), part(0, 1))
                second = jnp.where(lane < 96, part(1, 0), part(1, 1))
                picked = jnp.where(lane < 64, first, second)
                out_ref[level, q, pair * ROWS : (pair + 1) * ROWS, :] = picked.astype(BF16)
            rows = [sorted_ref[i, pl.ds(level * QUAD + q, 1), :].astype(F32) for i in range(2)]
            rows = jnp.concatenate(rows + [jnp.zeros((6, 128), F32)], axis=0)
            out_ref[level, q, 32:40, :] = rows.astype(BF16)
            return carry

        lax.fori_loop(0, LEVELS, pick, 0, unroll=True)
        emits[q].start()
    for copy in emits:
        copy.wait()


def sum_kernel(usage_ref, got_ref, avg_ref, square_ref, *rest):
    peer_refs = rest[:3]
    where_ref = rest[3]
    total_refs = rest[4:8]
    count_ref = rest[8]
    lane = lanes(8)
    block = lane // CH
    k = lane % CH
    for total in total_refs:
        total[...] = jnp.zeros_like(total)
    for o in range(OPTIONS):
        count_ref[o] = 0

    def invert(group, carry):
        at = pl.ds(pl.multiple_of(group * 8, 8), 8)
        index = got_ref[at, 32:40, :].astype(F32)
        for pair in range(2):
            rows = index[:, pair, :].astype(jnp.int32)
            for half in range(2):
                for tile in range(2):
                    place = half * 64 + (tile * 2 + block) * KEEP
                    held = take_lanes(rows, place)
                    for step in (8, 4, 2, 1):
                        probe = take_lanes(rows, place + step)
                        below = probe <= k
                        place = jnp.where(below, place + step, place)
                        held = jnp.where(below, probe, held)
                    found = jnp.where(held == k, place, -1)
                    where_ref[pair * 4 + half * 2 + tile, at, :] = found
        return carry

    lax.fori_loop(0, DEVICES // 8, invert, 0, unroll=4)

    def add(s, carry):
        for pair in range(2):
            values = got_ref[s, pair * ROWS : (pair + 1) * ROWS, :].astype(F32)
            for half in range(2):
                o = usage_ref[s * MINE + pair * 2 + half]
                count_ref[o] += 1
                rows = pl.ds(pl.multiple_of(o * ROWS, ROWS), ROWS)
                total = total_refs[pair * 2 + half]
                for tile in range(2):
                    index = jnp.broadcast_to(
                        where_ref[pair * 4 + half * 2 + tile, pl.ds(s, 1), :], (ROWS, 128)
                    )
                    spread = jnp.where(index >= 0, take_lanes(values, jnp.maximum(index, 0)), 0.0)
                    total[rows, tile * 128 : (tile + 1) * 128] += spread
        return carry

    lax.fori_loop(0, DEVICES, add, 0, unroll=16)

    squares = []
    for o in range(OPTIONS):
        at = slice(o * ROWS, (o + 1) * ROWS)
        summed = (total_refs[0][at, :] + total_refs[1][at, :]) + (
            total_refs[2][at, :] + total_refs[3][at, :]
        )
        average = summed / jnp.maximum(count_ref[o], 1).astype(F32)
        avg_ref[o // MINE, (o % MINE) * ROWS : (o % MINE + 1) * ROWS, :] = average.astype(BF16)
        square = average * average
        squares.append(jnp.sum(square[:, :128] + square[:, 128:], axis=0, keepdims=True))
    squares = jnp.sum(jnp.concatenate(squares, axis=0), axis=1, keepdims=True)
    square_ref[...] = jnp.broadcast_to(squares[None], square_ref.shape)
    for i, peer_ref in enumerate(peer_refs):
        peer_ref[...] = avg_ref[usage_ref[PATHS] ^ (i + 1)]


def clip_factor(square_ref):
    total = jnp.sum(square_ref[...], axis=0)
    entries = 4.0 * ROWS * WIDTH
    return jnp.minimum(1.0, 0.3 / jnp.sqrt(total / entries + 1e-06))


def reply_kernel(usage_ref, avg_ref, square_ref, table_ref, *rest):
    base_refs = rest[:4]
    out_any, factor_ref, fresh_ref, reply_ref, sems = rest[4:]
    factor_ref[...] = clip_factor(square_ref)
    for k in range(QUAD):
        owner = usage_ref[PATHS] ^ k
        delta = dot2(avg_ref[owner], table_ref)
        for i in range(MINE):
            module = owner * MINE + i
            at = slice(i * ROWS, (i + 1) * ROWS)
            change = (1.33 * factor_ref[pl.ds(module, 1), 0:1]) * delta[at, :]
            fresh = (base_refs[k][at, :] - change).astype(BF16)
            fresh_ref[pl.ds(pl.multiple_of(module * ROWS, ROWS), ROWS), :] = fresh

    chunks = sems.shape[0]
    targets = DEVICES // chunks

    def emit(c):
        at = pl.ds(c * targets, targets)
        return pltpu.make_async_copy(reply_ref.at[at], out_any.at[at], sems.at[c])

    def chunk(c, carry):
        for d in range(targets):
            target = c * targets + d
            for p in range(MINE):
                o = usage_ref[target * MINE + p]
                rows = pl.ds(pl.multiple_of(o * ROWS, ROWS), ROWS)
                reply_ref[target, p] = fresh_ref[rows, :]
        emit(c).start()
        return carry

    lax.fori_loop(0, chunks, chunk, 0)
    for c in range(chunks):
        emit(c).wait()


def owner_kernel(usage_ref, avg_ref, square_ref, table_ref, params_ref, momentum_ref, *rest):
    peer_refs = rest[:3]
    new_params_ref, new_momentum_ref, factor_ref = rest[3:]
    q = usage_ref[PATHS]
    factor_ref[...] = clip_factor(square_ref)
    for k in range(QUAD):
        at = pl.ds(pl.multiple_of((q ^ k) * COLS, COLS), COLS)
        average = avg_ref[q] if k == 0 else peer_refs[k - 1][...]
        delta = dot2(average, table_ref)
        for i in range(MINE):
            factor = factor_ref[pl.ds(q * MINE + i, 1), 0:1]
            clipped = delta[i * ROWS : (i + 1) * ROWS, :] * factor
            momentum = 0.9 * momentum_ref[i, :, at] + clipped
            new_momentum_ref[i, :, at] = momentum
            new = params_ref[i, :, at].astype(F32) - 0.7 * (clipped + 0.9 * momentum)
            new_params_ref[i, :, at] = new.astype(BF16)


def place_kernel(got_ref, out_ref, sems):
    copies = []
    for q in range(QUAD):
        for p in range(MINE):
            copies.append(
                pltpu.make_async_copy(
                    got_ref.at[:, q, p],
                    out_ref.at[p, :, :, pl.ds(q * COLS, COLS)],
                    sems.at[q * MINE + p],
                )
            )
    for copy in copies:
        copy.start()
    for copy in copies:
        copy.wait()


def call(kernel, out_shape, limit=VMEM_LIMIT, **kwargs):
    return pl.pallas_call(
        kernel,
        out_shape=out_shape,
        compiler_params=pltpu.CompilerParams(vmem_limit_bytes=limit),
        **kwargs,
    )


def shaped(shape, dtype):
    return jax.ShapeDtypeStruct(shape, dtype)


def swap(values, k):
    return lax.ppermute(values, "quad", [(i, i ^ k) for i in range(QUAD)])


def local(pseudo_grad, kept_index, usage, module_params, momentum):
    forward, inverse = dct_tables()
    smem = pl.BlockSpec(memory_space=pltpu.SMEM)
    vmem = pl.BlockSpec(memory_space=pltpu.VMEM)
    level, q = lax.axis_index("level"), lax.axis_index("quad")
    used = lax.dynamic_slice_in_dim(usage, level, 1, 1).reshape(PATHS)
    used = jnp.concatenate([used, jnp.full((8,), q, jnp.int32)])

    bases = call(
        base_kernel,
        [shaped((MINE * ROWS, COLS), F32)] * QUAD,
        in_specs=[smem, vmem, vmem],
        out_specs=[vmem] * QUAD,
    )(jnp.full((1,), q, jnp.int32), module_params, momentum)
    bases = [bases[0]] + [swap(bases[k], k) for k in range(1, QUAD)]

    anywhere = pl.BlockSpec(memory_space=pl.ANY)
    outgoing = call(
        pick_kernel,
        shaped((LEVELS, QUAD, SENT, 128), BF16),
        in_specs=[anywhere] * 3,
        out_specs=anywhere,
        scratch_shapes=[
            pltpu.VMEM((MINE, LEVELS, ROWS, WIDTH), BF16),
            pltpu.VMEM((MINE, LEVELS, 16, KEEP), jnp.int32),
            pltpu.VMEM((2, COLS, COLS), BF16),
            pltpu.VMEM((QUAD, MINE * LEVELS * ROWS, COLS), F32),
            pltpu.VMEM((2, LEVELS * QUAD, 128), jnp.int32),
            pltpu.VMEM((LEVELS, QUAD, SENT, 128), BF16),
            pltpu.SemaphoreType.DMA((2 + MINE + QUAD,)),
        ],
        limit=STREAM_LIMIT,
    )(pseudo_grad, kept_index, forward)
    got = lax.all_to_all(outgoing.reshape(DEVICES, SENT, 128), PATH, 0, 0, tiled=True)
    got, bases = lax.optimization_barrier((got, bases))

    average, squares, *pieces = call(
        sum_kernel,
        [shaped((QUAD, MINE * ROWS, COLS), BF16), shaped((16, OPTIONS, 128), F32)]
        + [shaped((MINE * ROWS, COLS), BF16)] * 3,
        in_specs=[smem, vmem],
        out_specs=[vmem] * 5,
        scratch_shapes=[pltpu.VMEM((8, DEVICES, 128), jnp.int32)]
        + [pltpu.VMEM((OPTIONS * ROWS, COLS), F32)] * 4
        + [pltpu.SMEM((OPTIONS,), jnp.int32)],
    )(used, got)
    squares = lax.all_to_all(squares, SQUARE_GROUP, 0, 0, tiled=True)

    replies = call(
        reply_kernel,
        shaped((DEVICES, MINE, ROWS, COLS), BF16),
        in_specs=[smem] + [vmem] * 7,
        out_specs=anywhere,
        scratch_shapes=[
            pltpu.VMEM((OPTIONS, 128), F32),
            pltpu.VMEM((OPTIONS * ROWS, COLS), BF16),
            pltpu.VMEM((DEVICES, MINE, ROWS, COLS), BF16),
            pltpu.SemaphoreType.DMA((CHUNKS,)),
        ],
        limit=STREAM_LIMIT,
    )(used, average, squares, inverse, *bases)
    returned = lax.all_to_all(replies, PATH, 0, 0, tiled=True)

    pieces, replies = lax.optimization_barrier((pieces, replies))
    pieces = [swap(piece, k + 1) for k, piece in enumerate(pieces)]

    new_params, new_momentum = call(
        owner_kernel,
        [shaped((MINE, ROWS, WIDTH), BF16), shaped((MINE, ROWS, WIDTH), F32)],
        in_specs=[smem] + [vmem] * 8,
        out_specs=[vmem] * 2,
        scratch_shapes=[pltpu.VMEM((OPTIONS, 128), F32)],
    )(used, average, squares, inverse, module_params, momentum, *pieces)

    path_params = call(
        place_kernel,
        shaped((MINE, LEVELS, ROWS, WIDTH), BF16),
        in_specs=[anywhere],
        out_specs=anywhere,
        scratch_shapes=[pltpu.SemaphoreType.DMA((QUAD * MINE,))],
    )(returned.reshape(LEVELS, QUAD, MINE, ROWS, COLS))
    return (new_params, new_momentum, path_params)


def solution(mesh):
    mesh = Mesh(mesh.devices.reshape(LEVELS, QUAD, 4), PATH + ("shard",))
    return jax.shard_map(
        local,
        mesh=mesh,
        in_specs=(
            P(PATH, None, "shard", None),
            P(PATH, None, None, None),
            P(),
            P(PATH, "shard", None),
            P(PATH, "shard", None),
        ),
        out_specs=(
            P(PATH, "shard", None),
            P(PATH, "shard", None),
            P(PATH, None, "shard", None),
        ),
        check_vma=False,
    )
```

```python
import functools
import math

import jax
import jax.numpy as jnp
import ml_dtypes
import numpy as np
from jax import lax
from jax.experimental import pallas as pl
from jax.experimental.pallas import tpu as pltpu
from jax.sharding import Mesh
from jax.sharding import PartitionSpec as P

CH = 64
KEEP = 16
LEVELS = 16
OPTIONS = 16
ROWS = 16
WIDTH = 1024
PATHS = 256
DEVICES = 64
MINE = 4
QUAD = 4
COLS = WIDTH // QUAD
SENT = 40
F32 = jnp.float32
BF16 = jnp.bfloat16
CHUNKS = 4
VMEM_LIMIT = 40 * 1024 * 1024
STREAM_LIMIT = 56 * 1024 * 1024
PATH = ("z", "half", "quad")
ROW = ("half", "quad")
DEPTH = 8
NEAR = (0, -1, 1, -2, 2)
FAR = (-3, 3, 4)
SQUARE_GROUP = ("quad", "shard")


def dct_tables():
    k = np.arange(CH)[:, None]
    n = np.arange(CH)[None, :]
    scale = np.where(k == 0, math.sqrt(1.0 / CH), math.sqrt(2.0 / CH))
    table = np.kron(np.eye(4), scale * np.cos(math.pi * (2.0 * n + 1.0) * k / (2.0 * CH)))
    high = table.astype(ml_dtypes.bfloat16)
    low = (table - high.astype(np.float64)).astype(ml_dtypes.bfloat16)
    inverse = np.stack([high, low])
    return np.ascontiguousarray(inverse.transpose(0, 2, 1)), inverse


def dot2(values, table_ref):
    return jnp.dot(values, table_ref[0], preferred_element_type=F32) + jnp.dot(
        values, table_ref[1], preferred_element_type=F32
    )


def take_lanes(values, index):
    return jnp.take_along_axis(values, index, axis=1, mode="promise_in_bounds")


def lanes(rows):
    return lax.broadcasted_iota(jnp.int32, (rows, 128), 1)


def base_kernel(q_ref, params_ref, momentum_ref, *out_refs):
    for k in range(QUAD):
        at = pl.ds(pl.multiple_of((q_ref[0] ^ k) * COLS, COLS), COLS)
        for i in range(MINE):
            base = params_ref[i, :, at].astype(F32) - 0.567 * momentum_ref[i, :, at]
            out_refs[k][i * ROWS : (i + 1) * ROWS, :] = base


def sort_groups(values):
    lane = lanes(values.shape[0])
    size = 2
    while size <= KEEP:
        distance = size // 2
        while distance >= 1:
            other = take_lanes(values, lane ^ distance)
            upward = (lane & size) == 0 if size < KEEP else lane >= 0
            first = (lane & distance) == 0
            keep_least = first == upward
            values = jnp.where(keep_least, jnp.minimum(values, other), jnp.maximum(values, other))
            distance //= 2
        size *= 2
    return values


def gather_kept(kept_ref, pair):
    rows = LEVELS * 16
    repeat = (lanes(KEEP) % KEEP == lax.broadcasted_iota(jnp.int32, (KEEP, 128), 0)).astype(BF16)
    block = lax.broadcasted_iota(jnp.int32, (rows, 128), 0) % 4
    lane = lanes(rows)
    total = jnp.zeros((rows, 128), F32)
    for half in range(2):
        kept = kept_ref[pair * 2 + half].reshape(rows, KEEP).astype(F32).astype(BF16)
        spread = jnp.dot(kept, repeat, preferred_element_type=F32)
        total = jnp.where(lane // KEEP == half * 4 + block, spread, total)
    row = lax.broadcasted_iota(jnp.int32, (LEVELS * QUAD, rows), 0)
    column = lax.broadcasted_iota(jnp.int32, (LEVELS * QUAD, rows), 1)
    fold = (column // 4 == row).astype(BF16)
    return jnp.dot(fold, total.astype(BF16), preferred_element_type=F32).astype(jnp.int32)


def pick_kernel(
    grad_any,
    kept_any,
    table_any,
    out_any,
    grad_ref,
    kept_ref,
    table_ref,
    spectrum_ref,
    sorted_ref,
    out_ref,
    sems,
):
    kept = pltpu.make_async_copy(kept_any, kept_ref, sems.at[0])
    table = pltpu.make_async_copy(table_any, table_ref, sems.at[1])
    grads = [
        pltpu.make_async_copy(grad_any.at[p], grad_ref.at[p], sems.at[2 + p]) for p in range(MINE)
    ]
    emits = [
        pltpu.make_async_copy(out_ref.at[:, q], out_any.at[:, q], sems.at[2 + MINE + q])
        for q in range(QUAD)
    ]
    for copy in [kept, table] + grads:
        copy.start()
    kept.wait()
    for pair in range(2):
        sorted_ref[pair] = sort_groups(gather_kept(kept_ref, pair))
    lane = lanes(ROWS)
    shift = ((lane // KEEP) % 2) * CH
    for copy in [table] + grads:
        copy.wait()

    for q in range(QUAD):
        grad = grad_ref[:, :, :, q * COLS : (q + 1) * COLS].reshape(MINE * LEVELS * ROWS, COLS)
        spectrum_ref[q] = dot2(grad, table_ref)

        def pick(level, carry):
            for pair in range(2):
                row = sorted_ref[pair, pl.ds(level * QUAD + q, 1), :]
                index = jnp.broadcast_to(row, (ROWS, 128)) + shift

                def part(half, tile):
                    start = ((pair * 2 + half) * LEVELS + level) * ROWS
                    rows = pl.ds(pl.multiple_of(start, ROWS), ROWS)
                    return take_lanes(spectrum_ref[q, rows, tile * 128 : (tile + 1) * 128], index)

                first = jnp.where(lane < 32, part(0, 0), part(0, 1))
                second = jnp.where(lane < 96, part(1, 0), part(1, 1))
                picked = jnp.where(lane < 64, first, second)
                out_ref[level, q, pair * ROWS : (pair + 1) * ROWS, :] = picked.astype(BF16)
            rows = [sorted_ref[i, pl.ds(level * QUAD + q, 1), :].astype(F32) for i in range(2)]
            rows = jnp.concatenate(rows + [jnp.zeros((6, 128), F32)], axis=0)
            out_ref[level, q, 32:40, :] = rows.astype(BF16)
            return carry

        lax.fori_loop(0, LEVELS, pick, 0, unroll=True)
        emits[q].start()
    for copy in emits:
        copy.wait()


def sum_kernel(usage_ref, got_ref, avg_ref, square_ref, *rest):
    peer_refs = rest[:3]
    where_ref = rest[3]
    total_refs = rest[4:8]
    count_ref = rest[8]
    lane = lanes(8)
    block = lane // CH
    k = lane % CH
    for total in total_refs:
        total[...] = jnp.zeros_like(total)
    for o in range(OPTIONS):
        count_ref[o] = 0

    def invert(group, carry):
        at = pl.ds(pl.multiple_of(group * 8, 8), 8)
        index = got_ref[at, 32:40, :].astype(F32)
        for pair in range(2):
            rows = index[:, pair, :].astype(jnp.int32)
            for half in range(2):
                for tile in range(2):
                    place = half * 64 + (tile * 2 + block) * KEEP
                    held = take_lanes(rows, place)
                    for step in (8, 4, 2, 1):
                        probe = take_lanes(rows, place + step)
                        below = probe <= k
                        place = jnp.where(below, place + step, place)
                        held = jnp.where(below, probe, held)
                    found = jnp.where(held == k, place, -1)
                    where_ref[pair * 4 + half * 2 + tile, at, :] = found
        return carry

    lax.fori_loop(0, DEVICES // 8, invert, 0, unroll=4)

    def add(s, carry):
        for pair in range(2):
            values = got_ref[s, pair * ROWS : (pair + 1) * ROWS, :].astype(F32)
            for half in range(2):
                o = usage_ref[s * MINE + pair * 2 + half]
                count_ref[o] += 1
                rows = pl.ds(pl.multiple_of(o * ROWS, ROWS), ROWS)
                total = total_refs[pair * 2 + half]
                for tile in range(2):
                    index = jnp.broadcast_to(
                        where_ref[pair * 4 + half * 2 + tile, pl.ds(s, 1), :], (ROWS, 128)
                    )
                    spread = jnp.where(index >= 0, take_lanes(values, jnp.maximum(index, 0)), 0.0)
                    total[rows, tile * 128 : (tile + 1) * 128] += spread
        return carry

    lax.fori_loop(0, DEVICES, add, 0, unroll=16)

    squares = []
    for o in range(OPTIONS):
        at = slice(o * ROWS, (o + 1) * ROWS)
        summed = (total_refs[0][at, :] + total_refs[1][at, :]) + (
            total_refs[2][at, :] + total_refs[3][at, :]
        )
        average = summed / jnp.maximum(count_ref[o], 1).astype(F32)
        avg_ref[o // MINE, (o % MINE) * ROWS : (o % MINE + 1) * ROWS, :] = average.astype(BF16)
        square = average * average
        squares.append(jnp.sum(square[:, :128] + square[:, 128:], axis=0, keepdims=True))
    squares = jnp.sum(jnp.concatenate(squares, axis=0), axis=1, keepdims=True)
    square_ref[...] = jnp.broadcast_to(squares[None], square_ref.shape)
    for i, peer_ref in enumerate(peer_refs):
        peer_ref[...] = avg_ref[usage_ref[PATHS] ^ (i + 1)]


def clip_factor(square_ref):
    total = jnp.sum(square_ref[...], axis=0)
    entries = 4.0 * ROWS * WIDTH
    return jnp.minimum(1.0, 0.3 / jnp.sqrt(total / entries + 1e-06))


def fresh_kernel(usage_ref, avg_ref, square_ref, table_ref, *rest):
    base_refs = rest[:4]
    fresh_ref, factor_ref = rest[4:]
    factor_ref[...] = clip_factor(square_ref)
    for k in range(QUAD):
        owner = usage_ref[PATHS] ^ k
        delta = dot2(avg_ref[owner], table_ref)
        for i in range(MINE):
            module = owner * MINE + i
            at = slice(i * ROWS, (i + 1) * ROWS)
            change = (1.33 * factor_ref[pl.ds(module, 1), 0:1]) * delta[at, :]
            fresh = (base_refs[k][at, :] - change).astype(BF16)
            fresh_ref[pl.ds(pl.multiple_of(module * ROWS, ROWS), ROWS), :] = fresh


def pack_kernel(steps, row_ref, *rest):
    block_refs = rest[: len(steps)]
    out_any, out_ref, sems = rest[len(steps) :]
    copies = []
    for b, step in enumerate(steps):
        origin = (row_ref[PATHS] + (step + DEPTH)) % DEPTH
        for target in range(8):
            for p in range(MINE):
                o = row_ref[origin * 32 + target * MINE + p]
                rows = pl.ds(pl.multiple_of(o * ROWS, ROWS), ROWS)
                out_ref[target, b, p] = block_refs[b][rows, :]
        copies.append(pltpu.make_async_copy(out_ref.at[:, b], out_any.at[:, b], sems.at[b]))
        copies[-1].start()
    for copy in copies:
        copy.wait()


def owner_kernel(usage_ref, avg_ref, square_ref, table_ref, params_ref, momentum_ref, *rest):
    peer_refs = rest[:3]
    new_params_ref, new_momentum_ref, factor_ref = rest[3:]
    q = usage_ref[PATHS]
    factor_ref[...] = clip_factor(square_ref)
    for k in range(QUAD):
        at = pl.ds(pl.multiple_of((q ^ k) * COLS, COLS), COLS)
        average = avg_ref[q] if k == 0 else peer_refs[k - 1][...]
        delta = dot2(average, table_ref)
        for i in range(MINE):
            factor = factor_ref[pl.ds(q * MINE + i, 1), 0:1]
            clipped = delta[i * ROWS : (i + 1) * ROWS, :] * factor
            momentum = 0.9 * momentum_ref[i, :, at] + clipped
            new_momentum_ref[i, :, at] = momentum
            new = params_ref[i, :, at].astype(F32) - 0.7 * (clipped + 0.9 * momentum)
            new_params_ref[i, :, at] = new.astype(BF16)


def place_kernel(steps, row_ref, got_ref, *rest):
    out_ref, sems = rest[-2:]
    copies = []
    for b, step in enumerate(steps):
        origin = (row_ref[PATHS] + (step + DEPTH)) % DEPTH
        for half in range(2):
            for q in range(QUAD):
                copies.append(
                    pltpu.make_async_copy(
                        got_ref.at[half * QUAD + q, b],
                        out_ref.at[:, origin * 2 + half, :, pl.ds(q * COLS, COLS)],
                        sems.at[len(copies)],
                    )
                )
    for copy in copies:
        copy.start()
    for copy in copies:
        copy.wait()


def call(kernel, out_shape, limit=VMEM_LIMIT, **kwargs):
    return pl.pallas_call(
        kernel,
        out_shape=out_shape,
        compiler_params=pltpu.CompilerParams(vmem_limit_bytes=limit),
        **kwargs,
    )


def shaped(shape, dtype):
    return jax.ShapeDtypeStruct(shape, dtype)


def swap(values, k):
    return lax.ppermute(values, "quad", [(i, i ^ k) for i in range(QUAD)])


def along(values, k):
    return lax.ppermute(values, "z", [(i, (i + k) % DEPTH) for i in range(DEPTH)])


def pack_row(steps, row, blocks):
    shape = (8, len(steps), MINE, ROWS, COLS)
    return call(
        functools.partial(pack_kernel, steps),
        shaped(shape, BF16),
        in_specs=[pl.BlockSpec(memory_space=pltpu.SMEM)]
        + [pl.BlockSpec(memory_space=pltpu.VMEM)] * len(steps),
        out_specs=pl.BlockSpec(memory_space=pltpu.HBM),
        scratch_shapes=[pltpu.VMEM(shape, BF16), pltpu.SemaphoreType.DMA((len(steps),))],
    )(row, *blocks)


def place_row(steps, row, got, rest):
    anywhere = pl.BlockSpec(memory_space=pl.ANY)
    return call(
        functools.partial(place_kernel, steps),
        shaped((MINE, LEVELS, ROWS, WIDTH), BF16),
        in_specs=[pl.BlockSpec(memory_space=pltpu.SMEM)] + [anywhere] * (1 + len(rest)),
        out_specs=anywhere,
        scratch_shapes=[pltpu.SemaphoreType.DMA((8 * len(steps),))],
        input_output_aliases={2: 0} if rest else {},
    )(row, got, *rest)


def local(pseudo_grad, kept_index, usage, module_params, momentum):
    forward, inverse = dct_tables()
    smem = pl.BlockSpec(memory_space=pltpu.SMEM)
    vmem = pl.BlockSpec(memory_space=pltpu.VMEM)
    z, half, q = lax.axis_index("z"), lax.axis_index("half"), lax.axis_index("quad")
    level = 2 * z + half
    used = lax.dynamic_slice_in_dim(usage, level, 1, 1).reshape(PATHS)
    used = jnp.concatenate([used, jnp.full((8,), q, jnp.int32)])
    row = lax.dynamic_slice_in_dim(usage, 32 * z, 32, 0).reshape(32, DEPTH, 2)
    row = lax.dynamic_index_in_dim(row, half, 2, keepdims=False).T.reshape(PATHS)
    row = jnp.concatenate([row, jnp.full((8,), z, jnp.int32)])

    bases = call(
        base_kernel,
        [shaped((MINE * ROWS, COLS), F32)] * QUAD,
        in_specs=[smem, vmem, vmem],
        out_specs=[vmem] * QUAD,
    )(jnp.full((1,), q, jnp.int32), module_params, momentum)
    bases = [bases[0]] + [swap(bases[k], k) for k in range(1, QUAD)]

    anywhere = pl.BlockSpec(memory_space=pl.ANY)
    outgoing = call(
        pick_kernel,
        shaped((LEVELS, QUAD, SENT, 128), BF16),
        in_specs=[anywhere] * 3,
        out_specs=anywhere,
        scratch_shapes=[
            pltpu.VMEM((MINE, LEVELS, ROWS, WIDTH), BF16),
            pltpu.VMEM((MINE, LEVELS, 16, KEEP), jnp.int32),
            pltpu.VMEM((2, COLS, COLS), BF16),
            pltpu.VMEM((QUAD, MINE * LEVELS * ROWS, COLS), F32),
            pltpu.VMEM((2, LEVELS * QUAD, 128), jnp.int32),
            pltpu.VMEM((LEVELS, QUAD, SENT, 128), BF16),
            pltpu.SemaphoreType.DMA((2 + MINE + QUAD,)),
        ],
        limit=STREAM_LIMIT,
    )(pseudo_grad, kept_index, forward)
    got = lax.all_to_all(outgoing.reshape(DEVICES, SENT, 128), PATH, 0, 0, tiled=True)
    got, bases, row = lax.optimization_barrier((got, bases, row))

    average, squares, *pieces = call(
        sum_kernel,
        [shaped((QUAD, MINE * ROWS, COLS), BF16), shaped((16, OPTIONS, 128), F32)]
        + [shaped((MINE * ROWS, COLS), BF16)] * 3,
        in_specs=[smem, vmem],
        out_specs=[vmem] * 5,
        scratch_shapes=[pltpu.VMEM((8, DEVICES, 128), jnp.int32)]
        + [pltpu.VMEM((OPTIONS * ROWS, COLS), F32)] * 4
        + [pltpu.SMEM((OPTIONS,), jnp.int32)],
    )(used, got)
    squares = lax.all_to_all(squares, SQUARE_GROUP, 0, 0, tiled=True)
    pieces = [swap(piece, k + 1) for k, piece in enumerate(pieces)]
    squares, pieces = lax.optimization_barrier((squares, pieces))

    fresh = call(
        fresh_kernel,
        shaped((OPTIONS * ROWS, COLS), BF16),
        in_specs=[smem] + [vmem] * 7,
        out_specs=vmem,
        scratch_shapes=[pltpu.VMEM((OPTIONS, 128), F32)],
    )(used, average, squares, inverse, *bases)
    before, after = [fresh], [fresh]
    for _ in range(2):
        before.append(along(before[-1], 1))
        after.append(along(after[-1], -1))
    packed = pack_row(NEAR, row, [fresh, before[1], after[1], before[2], after[2]])
    packed, before2, after2 = lax.optimization_barrier((packed, before[2], after[2]))
    near = lax.all_to_all(packed, ROW, 0, 0, tiled=True)
    before3, after3 = along(before2, 1), along(after2, -1)
    packed = pack_row(FAR, row, [before3, after3, along(before3, 1)])
    packed, near, pieces = lax.optimization_barrier((packed, near, pieces))
    far = lax.all_to_all(packed, ROW, 0, 0, tiled=True)

    new_params, new_momentum = call(
        owner_kernel,
        [shaped((MINE, ROWS, WIDTH), BF16), shaped((MINE, ROWS, WIDTH), F32)],
        in_specs=[smem] + [vmem] * 8,
        out_specs=[vmem] * 2,
        scratch_shapes=[pltpu.VMEM((OPTIONS, 128), F32)],
    )(used, average, squares, inverse, module_params, momentum, *pieces)

    path_params = place_row(NEAR, row, near, [])
    path_params = place_row(FAR, row, far, [path_params])
    return (new_params, new_momentum, path_params)


def solution(mesh):
    mesh = Mesh(mesh.devices.reshape(DEPTH, 2, QUAD, 4), PATH + ("shard",))
    return jax.shard_map(
        local,
        mesh=mesh,
        in_specs=(
            P(PATH, None, "shard", None),
            P(PATH, None, None, None),
            P(),
            P(PATH, "shard", None),
            P(PATH, "shard", None),
        ),
        out_specs=(
            P(PATH, "shard", None),
            P(PATH, "shard", None),
            P(PATH, None, "shard", None),
        ),
        check_vma=False,
    )
```

```python
import functools
import math

import jax
import jax.numpy as jnp
import ml_dtypes
import numpy as np
from jax import lax
from jax.experimental import pallas as pl
from jax.experimental.pallas import tpu as pltpu
from jax.sharding import Mesh
from jax.sharding import PartitionSpec as P

CH = 64
KEEP = 16
LEVELS = 16
OPTIONS = 16
ROWS = 16
WIDTH = 1024
PATHS = 256
DEVICES = 64
MINE = 4
QUAD = 4
COLS = WIDTH // QUAD
SENT = 40
F32 = jnp.float32
BF16 = jnp.bfloat16
CHUNKS = 4
VMEM_LIMIT = 40 * 1024 * 1024
STREAM_LIMIT = 56 * 1024 * 1024
PATH = ("z", "half", "quad")
ROW = ("half", "quad")
DEPTH = 8
NEAR = (0, -1, 1, -2, 2)
FAR = (-3, 3, 4)
SQUARE_GROUP = ("quad", "shard")


def dct_tables():
    k = np.arange(CH)[:, None]
    n = np.arange(CH)[None, :]
    scale = np.where(k == 0, math.sqrt(1.0 / CH), math.sqrt(2.0 / CH))
    table = np.kron(np.eye(4), scale * np.cos(math.pi * (2.0 * n + 1.0) * k / (2.0 * CH)))
    high = table.astype(ml_dtypes.bfloat16)
    low = (table - high.astype(np.float64)).astype(ml_dtypes.bfloat16)
    inverse = np.stack([high, low])
    return np.ascontiguousarray(inverse.transpose(0, 2, 1)), inverse


def dot2(values, table_ref):
    return jnp.dot(values, table_ref[0], preferred_element_type=F32) + jnp.dot(
        values, table_ref[1], preferred_element_type=F32
    )


def take_lanes(values, index):
    return jnp.take_along_axis(values, index, axis=1, mode="promise_in_bounds")


def lanes(rows):
    return lax.broadcasted_iota(jnp.int32, (rows, 128), 1)


def base_kernel(q_ref, params_ref, momentum_ref, *out_refs):
    for k in range(QUAD):
        at = pl.ds(pl.multiple_of((q_ref[0] ^ k) * COLS, COLS), COLS)
        for i in range(MINE):
            base = params_ref[i, :, at].astype(F32) - 0.567 * momentum_ref[i, :, at]
            out_refs[k][i * ROWS : (i + 1) * ROWS, :] = base


def sort_groups(values):
    lane = lanes(values.shape[0])
    size = 2
    while size <= KEEP:
        distance = size // 2
        while distance >= 1:
            other = take_lanes(values, lane ^ distance)
            upward = (lane & size) == 0 if size < KEEP else lane >= 0
            first = (lane & distance) == 0
            keep_least = first == upward
            values = jnp.where(keep_least, jnp.minimum(values, other), jnp.maximum(values, other))
            distance //= 2
        size *= 2
    return values


def gather_kept(kept_ref, pair):
    rows = LEVELS * 16
    repeat = (lanes(KEEP) % KEEP == lax.broadcasted_iota(jnp.int32, (KEEP, 128), 0)).astype(BF16)
    block = lax.broadcasted_iota(jnp.int32, (rows, 128), 0) % 4
    lane = lanes(rows)
    total = jnp.zeros((rows, 128), F32)
    for half in range(2):
        kept = kept_ref[pair * 2 + half].reshape(rows, KEEP).astype(F32).astype(BF16)
        spread = jnp.dot(kept, repeat, preferred_element_type=F32)
        total = jnp.where(lane // KEEP == half * 4 + block, spread, total)
    row = lax.broadcasted_iota(jnp.int32, (LEVELS * QUAD, rows), 0)
    column = lax.broadcasted_iota(jnp.int32, (LEVELS * QUAD, rows), 1)
    fold = (column // 4 == row).astype(BF16)
    return jnp.dot(fold, total.astype(BF16), preferred_element_type=F32).astype(jnp.int32)


def pick_kernel(
    grad_any,
    kept_any,
    table_any,
    out_any,
    grad_ref,
    kept_ref,
    table_ref,
    spectrum_ref,
    sorted_ref,
    out_ref,
    sems,
):
    kept = pltpu.make_async_copy(kept_any, kept_ref, sems.at[0])
    table = pltpu.make_async_copy(table_any, table_ref, sems.at[1])
    grads = [
        pltpu.make_async_copy(grad_any.at[p], grad_ref.at[p], sems.at[2 + p]) for p in range(MINE)
    ]
    emits = [
        pltpu.make_async_copy(out_ref.at[:, q], out_any.at[:, q], sems.at[2 + MINE + q])
        for q in range(QUAD)
    ]
    for copy in [kept, table] + grads:
        copy.start()
    kept.wait()
    for pair in range(2):
        sorted_ref[pair] = sort_groups(gather_kept(kept_ref, pair))
    lane = lanes(ROWS)
    shift = ((lane // KEEP) % 2) * CH
    for copy in [table] + grads:
        copy.wait()

    for q in range(QUAD):
        grad = grad_ref[:, :, :, q * COLS : (q + 1) * COLS].reshape(MINE * LEVELS * ROWS, COLS)
        spectrum_ref[q] = dot2(grad, table_ref)

        def pick(level, carry):
            for pair in range(2):
                row = sorted_ref[pair, pl.ds(level * QUAD + q, 1), :]
                index = jnp.broadcast_to(row, (ROWS, 128)) + shift

                def part(half, tile):
                    start = ((pair * 2 + half) * LEVELS + level) * ROWS
                    rows = pl.ds(pl.multiple_of(start, ROWS), ROWS)
                    return take_lanes(spectrum_ref[q, rows, tile * 128 : (tile + 1) * 128], index)

                first = jnp.where(lane < 32, part(0, 0), part(0, 1))
                second = jnp.where(lane < 96, part(1, 0), part(1, 1))
                picked = jnp.where(lane < 64, first, second)
                out_ref[level, q, pair * ROWS : (pair + 1) * ROWS, :] = picked.astype(BF16)
            rows = [sorted_ref[i, pl.ds(level * QUAD + q, 1), :].astype(F32) for i in range(2)]
            rows = jnp.concatenate(rows + [jnp.zeros((6, 128), F32)], axis=0)
            out_ref[level, q, 32:40, :] = rows.astype(BF16)
            return carry

        lax.fori_loop(0, LEVELS, pick, 0, unroll=True)
        emits[q].start()
    for copy in emits:
        copy.wait()


def sum_kernel(usage_ref, got_ref, avg_ref, square_ref, *rest):
    peer_refs = rest[:3]
    where_ref = rest[3]
    total_refs = rest[4:8]
    count_ref = rest[8]
    lane = lanes(8)
    block = lane // CH
    k = lane % CH
    for total in total_refs:
        total[...] = jnp.zeros_like(total)
    for o in range(OPTIONS):
        count_ref[o] = 0

    def invert(group, carry):
        at = pl.ds(pl.multiple_of(group * 8, 8), 8)
        index = got_ref[at, 32:40, :].astype(F32)
        for pair in range(2):
            rows = index[:, pair, :].astype(jnp.int32)
            for half in range(2):
                for tile in range(2):
                    place = half * 64 + (tile * 2 + block) * KEEP
                    held = take_lanes(rows, place)
                    for step in (8, 4, 2, 1):
                        probe = take_lanes(rows, place + step)
                        below = probe <= k
                        place = jnp.where(below, place + step, place)
                        held = jnp.where(below, probe, held)
                    found = jnp.where(held == k, place, -1)
                    where_ref[pair * 4 + half * 2 + tile, at, :] = found
        return carry

    lax.fori_loop(0, DEVICES // 8, invert, 0, unroll=4)

    def add(s, carry):
        for pair in range(2):
            values = got_ref[s, pair * ROWS : (pair + 1) * ROWS, :].astype(F32)
            for half in range(2):
                o = usage_ref[s * MINE + pair * 2 + half]
                count_ref[o] += 1
                rows = pl.ds(pl.multiple_of(o * ROWS, ROWS), ROWS)
                total = total_refs[pair * 2 + half]
                for tile in range(2):
                    index = jnp.broadcast_to(
                        where_ref[pair * 4 + half * 2 + tile, pl.ds(s, 1), :], (ROWS, 128)
                    )
                    spread = jnp.where(index >= 0, take_lanes(values, jnp.maximum(index, 0)), 0.0)
                    total[rows, tile * 128 : (tile + 1) * 128] += spread
        return carry

    lax.fori_loop(0, DEVICES, add, 0, unroll=16)

    squares = []
    for o in range(OPTIONS):
        at = slice(o * ROWS, (o + 1) * ROWS)
        summed = (total_refs[0][at, :] + total_refs[1][at, :]) + (
            total_refs[2][at, :] + total_refs[3][at, :]
        )
        average = summed / jnp.maximum(count_ref[o], 1).astype(F32)
        avg_ref[o // MINE, (o % MINE) * ROWS : (o % MINE + 1) * ROWS, :] = average.astype(BF16)
        square = average * average
        squares.append(jnp.sum(square[:, :128] + square[:, 128:], axis=0, keepdims=True))
    squares = jnp.sum(jnp.concatenate(squares, axis=0), axis=1, keepdims=True)
    diagonal = lax.broadcasted_iota(jnp.int32, (OPTIONS, 128), 0) == lanes(OPTIONS)
    squares = jnp.sum(jnp.where(diagonal, squares, 0.0), axis=0, keepdims=True)
    square_ref[...] = jnp.broadcast_to(squares[None], square_ref.shape)
    for i, peer_ref in enumerate(peer_refs):
        peer_ref[...] = avg_ref[usage_ref[PATHS] ^ (i + 1)]


def clip_factor(square_ref):
    total = jnp.sum(square_ref[...], axis=0)
    entries = 4.0 * ROWS * WIDTH
    factors = jnp.minimum(1.0, 0.3 / jnp.sqrt(total / entries + 1e-06))
    diagonal = lax.broadcasted_iota(jnp.int32, (OPTIONS, 128), 0) == lanes(OPTIONS)
    factors = jnp.sum(jnp.where(diagonal, factors, 0.0), axis=1, keepdims=True)
    return jnp.broadcast_to(factors, (OPTIONS, 128))


def fresh_kernel(usage_ref, avg_ref, square_ref, table_ref, *rest):
    base_refs = rest[:4]
    fresh_ref, factor_ref = rest[4:]
    factor_ref[...] = clip_factor(square_ref)
    for k in range(QUAD):
        owner = usage_ref[PATHS] ^ k
        delta = dot2(avg_ref[owner], table_ref)
        for i in range(MINE):
            module = owner * MINE + i
            at = slice(i * ROWS, (i + 1) * ROWS)
            change = (1.33 * factor_ref[pl.ds(module, 1), 0:1]) * delta[at, :]
            fresh = (base_refs[k][at, :] - change).astype(BF16)
            fresh_ref[pl.ds(pl.multiple_of(module * ROWS, ROWS), ROWS), :] = fresh


def neighbour(own, shift):
    chip = ((own >> 1) + (shift >> 1)) & 3
    return chip * 2 + ((own & 1) ^ (shift & 1))


def pack_kernel(steps, row_ref, *rest):
    block_refs, out_refs = rest[: len(steps)], rest[len(steps) :]
    for shift in range(8):
        target = neighbour(row_ref[PATHS + 1], shift)
        for b, step in enumerate(steps):
            origin = (row_ref[PATHS] + (step + DEPTH)) % DEPTH
            for p in range(MINE):
                o = row_ref[origin * 32 + target * MINE + p]
                rows = pl.ds(pl.multiple_of(o * ROWS, ROWS), ROWS)
                out_refs[shift][b, p] = block_refs[b][rows, :]


def pack_all_kernel(steps, first, row_ref, *rest):
    block_refs = rest[: len(steps)]
    out_any, out_ref, sems = rest[-3:]
    copies = []
    for b, step in enumerate(steps):
        origin = (row_ref[PATHS] + (step + DEPTH)) % DEPTH
        for target in range(8):
            for p in range(MINE):
                o = row_ref[origin * 32 + target * MINE + p]
                rows = pl.ds(pl.multiple_of(o * ROWS, ROWS), ROWS)
                out_ref[target, b, p] = block_refs[b][rows, :]
        copies.append(pltpu.make_async_copy(out_ref.at[:, b], out_any.at[:, first + b], sems.at[b]))
        copies[-1].start()
    for copy in copies:
        copy.wait()


def owner_kernel(usage_ref, avg_ref, square_ref, table_ref, params_ref, momentum_ref, *rest):
    peer_refs = rest[:3]
    new_params_ref, new_momentum_ref, factor_ref = rest[3:]
    q = usage_ref[PATHS]
    factor_ref[...] = clip_factor(square_ref)
    for k in range(QUAD):
        at = pl.ds(pl.multiple_of((q ^ k) * COLS, COLS), COLS)
        average = avg_ref[q] if k == 0 else peer_refs[k - 1][...]
        delta = dot2(average, table_ref)
        for i in range(MINE):
            factor = factor_ref[pl.ds(q * MINE + i, 1), 0:1]
            clipped = delta[i * ROWS : (i + 1) * ROWS, :] * factor
            momentum = 0.9 * momentum_ref[i, :, at] + clipped
            new_momentum_ref[i, :, at] = momentum
            new = params_ref[i, :, at].astype(F32) - 0.7 * (clipped + 0.9 * momentum)
            new_params_ref[i, :, at] = new.astype(BF16)


def place_kernel(steps, row_ref, *rest):
    got_refs = rest[:8]
    out_ref, sems = rest[-2:]
    copies = []
    for shift, got_ref in enumerate(got_refs):
        source = neighbour(row_ref[PATHS + 1], 8 - (shift & 6) + (shift & 1))
        columns = pl.ds(pl.multiple_of((source & 3) * COLS, COLS), COLS)
        for b, step in enumerate(steps):
            origin = (row_ref[PATHS] + (step + DEPTH)) % DEPTH
            level = origin * 2 + (source >> 2)
            copies.append(
                pltpu.make_async_copy(
                    got_ref.at[b], out_ref.at[:, level, :, columns], sems.at[len(copies)]
                )
            )
    for copy in copies:
        copy.start()
    for copy in copies:
        copy.wait()


def place_all_kernel(steps, row_ref, got_ref, *rest):
    out_ref, sems = rest[-2:]
    copies = []
    for b, step in enumerate(steps):
        origin = (row_ref[PATHS] + (step + DEPTH)) % DEPTH
        for half in range(2):
            for q in range(QUAD):
                copies.append(
                    pltpu.make_async_copy(
                        got_ref.at[half * QUAD + q, b],
                        out_ref.at[:, origin * 2 + half, :, pl.ds(q * COLS, COLS)],
                        sems.at[len(copies)],
                    )
                )
    for copy in copies:
        copy.start()
    for copy in copies:
        copy.wait()


def call(kernel, out_shape, limit=VMEM_LIMIT, **kwargs):
    return pl.pallas_call(
        kernel,
        out_shape=out_shape,
        compiler_params=pltpu.CompilerParams(vmem_limit_bytes=limit),
        **kwargs,
    )


def shaped(shape, dtype):
    return jax.ShapeDtypeStruct(shape, dtype)


def swap(values, k):
    return lax.ppermute(values, "quad", [(i, i ^ k) for i in range(QUAD)])


def along(values, k):
    return lax.ppermute(values, "z", [(i, (i + k) % DEPTH) for i in range(DEPTH)])


def pack_all(steps, row, blocks, first, rest):
    shape = (8, len(steps), MINE, ROWS, COLS)
    return call(
        functools.partial(pack_all_kernel, steps, first),
        shaped((8, len(NEAR), MINE, ROWS, COLS), BF16),
        in_specs=[pl.BlockSpec(memory_space=pltpu.SMEM)]
        + [pl.BlockSpec(memory_space=pltpu.VMEM)] * len(steps)
        + [pl.BlockSpec(memory_space=pltpu.HBM)] * len(rest),
        out_specs=pl.BlockSpec(memory_space=pltpu.HBM),
        scratch_shapes=[pltpu.VMEM(shape, BF16), pltpu.SemaphoreType.DMA((len(steps),))],
        input_output_aliases={1 + len(steps): 0} if rest else {},
    )(row, *blocks, *rest)


def pack_row(steps, row, blocks):
    vmem = pl.BlockSpec(memory_space=pltpu.VMEM)
    return call(
        functools.partial(pack_kernel, steps),
        [shaped((len(steps), MINE, ROWS, COLS), BF16)] * 8,
        in_specs=[pl.BlockSpec(memory_space=pltpu.SMEM)] + [vmem] * len(steps),
        out_specs=[vmem] * 8,
    )(row, *blocks)


def exchange_row(packed):
    got = [packed[0]]
    for shift in range(1, 8):
        pairs = [(i, neighbour(i, shift)) for i in range(8)]
        got.append(lax.ppermute(packed[shift], ROW, pairs))
    return got


def place_row(kernel, steps, row, got, rest):
    anywhere = pl.BlockSpec(memory_space=pl.ANY)
    return call(
        functools.partial(kernel, steps),
        shaped((MINE, LEVELS, ROWS, WIDTH), BF16),
        in_specs=[pl.BlockSpec(memory_space=pltpu.SMEM)] + [anywhere] * len(got + rest),
        out_specs=anywhere,
        scratch_shapes=[pltpu.SemaphoreType.DMA((8 * len(steps),))],
        input_output_aliases={1 + len(got): 0} if rest else {},
    )(row, *got, *rest)


def local(pseudo_grad, kept_index, usage, module_params, momentum):
    forward, inverse = dct_tables()
    smem = pl.BlockSpec(memory_space=pltpu.SMEM)
    vmem = pl.BlockSpec(memory_space=pltpu.VMEM)
    z, half, q = lax.axis_index("z"), lax.axis_index("half"), lax.axis_index("quad")
    level = 2 * z + half
    used = lax.dynamic_slice_in_dim(usage, level, 1, 1).reshape(PATHS)
    used = jnp.concatenate([used, jnp.full((8,), q, jnp.int32)])
    row = lax.dynamic_slice_in_dim(usage, 32 * z, 32, 0).reshape(32, DEPTH, 2)
    row = lax.dynamic_index_in_dim(row, half, 2, keepdims=False).T.reshape(PATHS)
    place = jnp.where(jnp.arange(8) == 0, z, half * QUAD + q).astype(jnp.int32)
    row = jnp.concatenate([row, place])

    bases = call(
        base_kernel,
        [shaped((MINE * ROWS, COLS), F32)] * QUAD,
        in_specs=[smem, vmem, vmem],
        out_specs=[vmem] * QUAD,
    )(jnp.full((1,), q, jnp.int32), module_params, momentum)
    bases = [bases[0]] + [swap(bases[k], k) for k in range(1, QUAD)]

    anywhere = pl.BlockSpec(memory_space=pl.ANY)
    outgoing = call(
        pick_kernel,
        shaped((LEVELS, QUAD, SENT, 128), BF16),
        in_specs=[anywhere] * 3,
        out_specs=anywhere,
        scratch_shapes=[
            pltpu.VMEM((MINE, LEVELS, ROWS, WIDTH), BF16),
            pltpu.VMEM((MINE, LEVELS, 16, KEEP), jnp.int32),
            pltpu.VMEM((2, COLS, COLS), BF16),
            pltpu.VMEM((QUAD, MINE * LEVELS * ROWS, COLS), F32),
            pltpu.VMEM((2, LEVELS * QUAD, 128), jnp.int32),
            pltpu.VMEM((LEVELS, QUAD, SENT, 128), BF16),
            pltpu.SemaphoreType.DMA((2 + MINE + QUAD,)),
        ],
        limit=STREAM_LIMIT,
    )(pseudo_grad, kept_index, forward)
    got = lax.all_to_all(outgoing.reshape(DEVICES, SENT, 128), PATH, 0, 0, tiled=True)
    got, bases, row = lax.optimization_barrier((got, bases, row))

    average, squares, *pieces = call(
        sum_kernel,
        [shaped((QUAD, MINE * ROWS, COLS), BF16), shaped((16, 1, 128), F32)]
        + [shaped((MINE * ROWS, COLS), BF16)] * 3,
        in_specs=[smem, vmem],
        out_specs=[vmem] * 5,
        scratch_shapes=[pltpu.VMEM((8, DEVICES, 128), jnp.int32)]
        + [pltpu.VMEM((OPTIONS * ROWS, COLS), F32)] * 4
        + [pltpu.SMEM((OPTIONS,), jnp.int32)],
    )(used, got)
    squares = lax.all_to_all(squares, SQUARE_GROUP, 0, 0, tiled=True)

    fresh = call(
        fresh_kernel,
        shaped((OPTIONS * ROWS, COLS), BF16),
        in_specs=[smem] + [vmem] * 7,
        out_specs=vmem,
        scratch_shapes=[pltpu.VMEM((OPTIONS, 128), F32)],
    )(used, average, squares, inverse, *bases)
    before, after = [fresh], [fresh]
    for _ in range(2):
        before.append(along(before[-1], 1))
        after.append(along(after[-1], -1))
    pieces, _ = lax.optimization_barrier((pieces, fresh))
    pieces = [swap(piece, k + 1) for k, piece in enumerate(pieces)]
    packed = pack_all(NEAR[:3], row, [fresh, before[1], after[1]], 0, [])
    packed, pieces = lax.optimization_barrier((packed, pieces))
    packed = pack_all(NEAR[3:], row, [before[2], after[2]], 3, [packed])
    packed, before2, after2 = lax.optimization_barrier((packed, before[2], after[2]))
    near = lax.all_to_all(packed, ROW, 0, 0, tiled=True)
    before3, after3 = along(before2, 1), along(after2, -1)
    far = exchange_row(pack_row(FAR, row, [before3, after3, along(before3, 1)]))

    new_params, new_momentum = call(
        owner_kernel,
        [shaped((MINE, ROWS, WIDTH), BF16), shaped((MINE, ROWS, WIDTH), F32)],
        in_specs=[smem] + [vmem] * 8,
        out_specs=[vmem] * 2,
        scratch_shapes=[pltpu.VMEM((OPTIONS, 128), F32)],
    )(used, average, squares, inverse, module_params, momentum, *pieces)

    path_params = place_row(place_all_kernel, NEAR, row, [near], [])
    path_params = place_row(place_kernel, FAR, row, far, [path_params])
    return (new_params, new_momentum, path_params)


def solution(mesh):
    mesh = Mesh(mesh.devices.reshape(DEPTH, 2, QUAD, 4), PATH + ("shard",))
    return jax.shard_map(
        local,
        mesh=mesh,
        in_specs=(
            P(PATH, None, "shard", None),
            P(PATH, None, None, None),
            P(),
            P(PATH, "shard", None),
            P(PATH, "shard", None),
        ),
        out_specs=(
            P(PATH, "shard", None),
            P(PATH, "shard", None),
            P(PATH, None, "shard", None),
        ),
        check_vma=False,
    )
```

```python
import functools
import math

import jax
import jax.numpy as jnp
import ml_dtypes
import numpy as np
from jax import lax
from jax.experimental import pallas as pl
from jax.experimental.pallas import tpu as pltpu
from jax.sharding import Mesh
from jax.sharding import PartitionSpec as P

CH = 64
KEEP = 16
LEVELS = 16
OPTIONS = 16
ROWS = 16
WIDTH = 1024
PATHS = 256
DEVICES = 64
MINE = 4
QUAD = 4
COLS = WIDTH // QUAD
SENT = 40
F32 = jnp.float32
BF16 = jnp.bfloat16
CHUNKS = 4
VMEM_LIMIT = 40 * 1024 * 1024
STREAM_LIMIT = 56 * 1024 * 1024
PATH = ("z", "half", "quad")
ROW = ("half", "quad")
DEPTH = 8
NEAR = (0, -1, 1, -2, 2)
FAR = (-3, 3, 4)
SQUARE_GROUP = ("quad", "shard")


def dct_tables():
    k = np.arange(CH)[:, None]
    n = np.arange(CH)[None, :]
    scale = np.where(k == 0, math.sqrt(1.0 / CH), math.sqrt(2.0 / CH))
    table = np.kron(np.eye(4), scale * np.cos(math.pi * (2.0 * n + 1.0) * k / (2.0 * CH)))
    high = table.astype(ml_dtypes.bfloat16)
    low = (table - high.astype(np.float64)).astype(ml_dtypes.bfloat16)
    inverse = np.stack([high, low])
    return np.ascontiguousarray(inverse.transpose(0, 2, 1)), inverse


def dot2(values, table_ref):
    return jnp.dot(values, table_ref[0], preferred_element_type=F32) + jnp.dot(
        values, table_ref[1], preferred_element_type=F32
    )


def take_lanes(values, index):
    return jnp.take_along_axis(values, index, axis=1, mode="promise_in_bounds")


def lanes(rows):
    return lax.broadcasted_iota(jnp.int32, (rows, 128), 1)


def base_kernel(q_ref, params_ref, momentum_ref, *out_refs):
    for k in range(QUAD):
        at = pl.ds(pl.multiple_of((q_ref[0] ^ k) * COLS, COLS), COLS)
        for i in range(MINE):
            base = params_ref[i, :, at].astype(F32) - 0.567 * momentum_ref[i, :, at]
            out_refs[k][i * ROWS : (i + 1) * ROWS, :] = base


def sort_groups(values):
    lane = lanes(values.shape[0])
    size = 2
    while size <= KEEP:
        distance = size // 2
        while distance >= 1:
            other = take_lanes(values, lane ^ distance)
            upward = (lane & size) == 0 if size < KEEP else lane >= 0
            first = (lane & distance) == 0
            keep_least = first == upward
            values = jnp.where(keep_least, jnp.minimum(values, other), jnp.maximum(values, other))
            distance //= 2
        size *= 2
    return values


def gather_kept(kept_ref, pair):
    rows = LEVELS * 16
    repeat = (lanes(KEEP) % KEEP == lax.broadcasted_iota(jnp.int32, (KEEP, 128), 0)).astype(BF16)
    block = lax.broadcasted_iota(jnp.int32, (rows, 128), 0) % 4
    lane = lanes(rows)
    total = jnp.zeros((rows, 128), F32)
    for half in range(2):
        kept = kept_ref[pair * 2 + half].reshape(rows, KEEP).astype(F32).astype(BF16)
        spread = jnp.dot(kept, repeat, preferred_element_type=F32)
        total = jnp.where(lane // KEEP == half * 4 + block, spread, total)
    row = lax.broadcasted_iota(jnp.int32, (LEVELS * QUAD, rows), 0)
    column = lax.broadcasted_iota(jnp.int32, (LEVELS * QUAD, rows), 1)
    fold = (column // 4 == row).astype(BF16)
    return jnp.dot(fold, total.astype(BF16), preferred_element_type=F32).astype(jnp.int32)


def pick_kernel(
    grad_any,
    kept_any,
    table_any,
    out_any,
    grad_ref,
    kept_ref,
    table_ref,
    spectrum_ref,
    sorted_ref,
    out_ref,
    sems,
):
    kept = pltpu.make_async_copy(kept_any, kept_ref, sems.at[0])
    table = pltpu.make_async_copy(table_any, table_ref, sems.at[1])
    grads = [
        pltpu.make_async_copy(grad_any.at[p], grad_ref.at[p], sems.at[2 + p]) for p in range(MINE)
    ]
    emits = [
        pltpu.make_async_copy(out_ref.at[:, q], out_any.at[:, q], sems.at[2 + MINE + q])
        for q in range(QUAD)
    ]
    for copy in [kept, table] + grads:
        copy.start()
    kept.wait()
    for pair in range(2):
        sorted_ref[pair] = sort_groups(gather_kept(kept_ref, pair))
    lane = lanes(ROWS)
    shift = ((lane // KEEP) % 2) * CH
    for copy in [table] + grads:
        copy.wait()

    for q in range(QUAD):
        grad = grad_ref[:, :, :, q * COLS : (q + 1) * COLS].reshape(MINE * LEVELS * ROWS, COLS)
        spectrum_ref[q] = dot2(grad, table_ref)

        def pick(level, carry):
            for pair in range(2):
                row = sorted_ref[pair, pl.ds(level * QUAD + q, 1), :]
                index = jnp.broadcast_to(row, (ROWS, 128)) + shift

                def part(half, tile):
                    start = ((pair * 2 + half) * LEVELS + level) * ROWS
                    rows = pl.ds(pl.multiple_of(start, ROWS), ROWS)
                    return take_lanes(spectrum_ref[q, rows, tile * 128 : (tile + 1) * 128], index)

                first = jnp.where(lane < 32, part(0, 0), part(0, 1))
                second = jnp.where(lane < 96, part(1, 0), part(1, 1))
                picked = jnp.where(lane < 64, first, second)
                out_ref[level, q, pair * ROWS : (pair + 1) * ROWS, :] = picked.astype(BF16)
            rows = [sorted_ref[i, pl.ds(level * QUAD + q, 1), :].astype(F32) for i in range(2)]
            rows = jnp.concatenate(rows + [jnp.zeros((6, 128), F32)], axis=0)
            out_ref[level, q, 32:40, :] = rows.astype(BF16)
            return carry

        lax.fori_loop(0, LEVELS, pick, 0, unroll=True)
        emits[q].start()
    for copy in emits:
        copy.wait()


def sum_kernel(usage_ref, got_ref, avg_ref, square_ref, *rest):
    peer_refs = rest[:3]
    where_ref = rest[3]
    total_refs = rest[4:8]
    count_ref = rest[8]
    lane = lanes(8)
    block = lane // CH
    k = lane % CH
    for total in total_refs:
        total[...] = jnp.zeros_like(total)
    for o in range(OPTIONS):
        count_ref[o] = 0

    def invert(group, carry):
        at = pl.ds(pl.multiple_of(group * 8, 8), 8)
        index = got_ref[at, 32:40, :].astype(F32)
        for pair in range(2):
            rows = index[:, pair, :].astype(jnp.int32)
            for half in range(2):
                for tile in range(2):
                    place = half * 64 + (tile * 2 + block) * KEEP
                    held = take_lanes(rows, place)
                    for step in (8, 4, 2, 1):
                        probe = take_lanes(rows, place + step)
                        below = probe <= k
                        place = jnp.where(below, place + step, place)
                        held = jnp.where(below, probe, held)
                    found = jnp.where(held == k, place, -1)
                    where_ref[pair * 4 + half * 2 + tile, at, :] = found
        return carry

    lax.fori_loop(0, DEVICES // 8, invert, 0, unroll=4)

    def add(s, carry):
        for pair in range(2):
            values = got_ref[s, pair * ROWS : (pair + 1) * ROWS, :].astype(F32)
            for half in range(2):
                o = usage_ref[s * MINE + pair * 2 + half]
                count_ref[o] += 1
                rows = pl.ds(pl.multiple_of(o * ROWS, ROWS), ROWS)
                total = total_refs[pair * 2 + half]
                for tile in range(2):
                    index = jnp.broadcast_to(
                        where_ref[pair * 4 + half * 2 + tile, pl.ds(s, 1), :], (ROWS, 128)
                    )
                    spread = jnp.where(index >= 0, take_lanes(values, jnp.maximum(index, 0)), 0.0)
                    total[rows, tile * 128 : (tile + 1) * 128] += spread
        return carry

    lax.fori_loop(0, DEVICES, add, 0, unroll=16)

    squares = []
    for o in range(OPTIONS):
        at = slice(o * ROWS, (o + 1) * ROWS)
        summed = (total_refs[0][at, :] + total_refs[1][at, :]) + (
            total_refs[2][at, :] + total_refs[3][at, :]
        )
        average = summed / jnp.maximum(count_ref[o], 1).astype(F32)
        avg_ref[o // MINE, (o % MINE) * ROWS : (o % MINE + 1) * ROWS, :] = average.astype(BF16)
        square = average * average
        squares.append(jnp.sum(square[:, :128] + square[:, 128:], axis=0, keepdims=True))
    squares = jnp.sum(jnp.concatenate(squares, axis=0), axis=1, keepdims=True)
    diagonal = lax.broadcasted_iota(jnp.int32, (OPTIONS, 128), 0) == lanes(OPTIONS)
    squares = jnp.sum(jnp.where(diagonal, squares, 0.0), axis=0, keepdims=True)
    square_ref[...] = jnp.broadcast_to(squares[None], square_ref.shape)
    for i, peer_ref in enumerate(peer_refs):
        peer_ref[...] = avg_ref[usage_ref[PATHS] ^ (i + 1)]


def clip_factor(square_ref):
    total = jnp.sum(square_ref[...], axis=0)
    entries = 4.0 * ROWS * WIDTH
    factors = jnp.minimum(1.0, 0.3 / jnp.sqrt(total / entries + 1e-06))
    diagonal = lax.broadcasted_iota(jnp.int32, (OPTIONS, 128), 0) == lanes(OPTIONS)
    factors = jnp.sum(jnp.where(diagonal, factors, 0.0), axis=1, keepdims=True)
    return jnp.broadcast_to(factors, (OPTIONS, 128))


def fresh_kernel(usage_ref, avg_ref, square_ref, table_ref, *rest):
    base_refs = rest[:4]
    fresh_ref, factor_ref = rest[4:]
    factor_ref[...] = clip_factor(square_ref)
    for k in range(QUAD):
        owner = usage_ref[PATHS] ^ k
        delta = dot2(avg_ref[owner], table_ref)
        for i in range(MINE):
            module = owner * MINE + i
            at = slice(i * ROWS, (i + 1) * ROWS)
            change = (1.33 * factor_ref[pl.ds(module, 1), 0:1]) * delta[at, :]
            fresh = (base_refs[k][at, :] - change).astype(BF16)
            fresh_ref[pl.ds(pl.multiple_of(module * ROWS, ROWS), ROWS), :] = fresh


def neighbour(own, shift):
    chip = ((own >> 1) + (shift >> 1)) & 3
    return chip * 2 + ((own & 1) ^ (shift & 1))


def pack_kernel(steps, row_ref, *rest):
    block_refs, out_refs = rest[: len(steps)], rest[len(steps) :]
    for shift in range(8):
        target = neighbour(row_ref[PATHS + 1], shift)
        for b, step in enumerate(steps):
            origin = (row_ref[PATHS] + (step + DEPTH)) % DEPTH
            for p in range(MINE):
                o = row_ref[origin * 32 + target * MINE + p]
                rows = pl.ds(pl.multiple_of(o * ROWS, ROWS), ROWS)
                out_refs[shift][b, p] = block_refs[b][rows, :]


def pack_all_kernel(steps, first, row_ref, *rest):
    block_refs = rest[: len(steps)]
    out_any, out_ref, sems = rest[-3:]
    copies = []
    for b, step in enumerate(steps):
        origin = (row_ref[PATHS] + (step + DEPTH)) % DEPTH
        for target in range(8):
            for p in range(MINE):
                o = row_ref[origin * 32 + target * MINE + p]
                rows = pl.ds(pl.multiple_of(o * ROWS, ROWS), ROWS)
                out_ref[target, b, p] = block_refs[b][rows, :]
        copies.append(pltpu.make_async_copy(out_ref.at[:, b], out_any.at[:, first + b], sems.at[b]))
        copies[-1].start()
    for copy in copies:
        copy.wait()


def owner_kernel(usage_ref, avg_ref, square_ref, table_ref, params_ref, momentum_ref, *rest):
    peer_refs = rest[:3]
    new_params_ref, new_momentum_ref, factor_ref = rest[3:]
    q = usage_ref[PATHS]
    factor_ref[...] = clip_factor(square_ref)
    for k in range(QUAD):
        at = pl.ds(pl.multiple_of((q ^ k) * COLS, COLS), COLS)
        average = avg_ref[q] if k == 0 else peer_refs[k - 1][...]
        delta = dot2(average, table_ref)
        for i in range(MINE):
            factor = factor_ref[pl.ds(q * MINE + i, 1), 0:1]
            clipped = delta[i * ROWS : (i + 1) * ROWS, :] * factor
            momentum = 0.9 * momentum_ref[i, :, at] + clipped
            new_momentum_ref[i, :, at] = momentum
            new = params_ref[i, :, at].astype(F32) - 0.7 * (clipped + 0.9 * momentum)
            new_params_ref[i, :, at] = new.astype(BF16)


def place_kernel(steps, row_ref, *rest):
    got_refs = rest[:8]
    out_ref, sems = rest[-2:]
    copies = []
    for shift, got_ref in enumerate(got_refs):
        source = neighbour(row_ref[PATHS + 1], 8 - (shift & 6) + (shift & 1))
        columns = pl.ds(pl.multiple_of((source & 3) * COLS, COLS), COLS)
        for b, step in enumerate(steps):
            origin = (row_ref[PATHS] + (step + DEPTH)) % DEPTH
            level = origin * 2 + (source >> 2)
            copies.append(
                pltpu.make_async_copy(
                    got_ref.at[b], out_ref.at[:, level, :, columns], sems.at[len(copies)]
                )
            )
    for copy in copies:
        copy.start()
    for copy in copies:
        copy.wait()


def place_all_kernel(steps, row_ref, got_ref, *rest):
    out_ref, sems = rest[-2:]
    copies = []
    for b, step in enumerate(steps):
        origin = (row_ref[PATHS] + (step + DEPTH)) % DEPTH
        for half in range(2):
            for q in range(QUAD):
                copies.append(
                    pltpu.make_async_copy(
                        got_ref.at[half * QUAD + q, b],
                        out_ref.at[:, origin * 2 + half, :, pl.ds(q * COLS, COLS)],
                        sems.at[len(copies)],
                    )
                )
    for copy in copies:
        copy.start()
    for copy in copies:
        copy.wait()


def call(kernel, out_shape, limit=VMEM_LIMIT, **kwargs):
    return pl.pallas_call(
        kernel,
        out_shape=out_shape,
        compiler_params=pltpu.CompilerParams(vmem_limit_bytes=limit),
        **kwargs,
    )


def shaped(shape, dtype):
    return jax.ShapeDtypeStruct(shape, dtype)


def swap(values, k):
    return lax.ppermute(values, "quad", [(i, i ^ k) for i in range(QUAD)])


def along(values, k):
    return lax.ppermute(values, "z", [(i, (i + k) % DEPTH) for i in range(DEPTH)])


def pack_all(steps, row, blocks, first, rest):
    shape = (8, len(steps), MINE, ROWS, COLS)
    return call(
        functools.partial(pack_all_kernel, steps, first),
        shaped((8, len(NEAR), MINE, ROWS, COLS), BF16),
        in_specs=[pl.BlockSpec(memory_space=pltpu.SMEM)]
        + [pl.BlockSpec(memory_space=pltpu.VMEM)] * len(steps)
        + [pl.BlockSpec(memory_space=pltpu.HBM)] * len(rest),
        out_specs=pl.BlockSpec(memory_space=pltpu.HBM),
        scratch_shapes=[pltpu.VMEM(shape, BF16), pltpu.SemaphoreType.DMA((len(steps),))],
        input_output_aliases={1 + len(steps): 0} if rest else {},
    )(row, *blocks, *rest)


def pack_row(steps, row, blocks):
    vmem = pl.BlockSpec(memory_space=pltpu.VMEM)
    return call(
        functools.partial(pack_kernel, steps),
        [shaped((len(steps), MINE, ROWS, COLS), BF16)] * 8,
        in_specs=[pl.BlockSpec(memory_space=pltpu.SMEM)] + [vmem] * len(steps),
        out_specs=[vmem] * 8,
    )(row, *blocks)


def exchange_row(packed):
    got = {0: packed[0]}
    for shift in (4, 5, 2, 6, 3, 7, 1):
        pairs = [(i, neighbour(i, shift)) for i in range(8)]
        got[shift] = lax.ppermute(packed[shift], ROW, pairs)
    return [got[shift] for shift in range(8)]


def place_row(kernel, steps, row, got, rest):
    anywhere = pl.BlockSpec(memory_space=pl.ANY)
    return call(
        functools.partial(kernel, steps),
        shaped((MINE, LEVELS, ROWS, WIDTH), BF16),
        in_specs=[pl.BlockSpec(memory_space=pltpu.SMEM)] + [anywhere] * len(got + rest),
        out_specs=anywhere,
        scratch_shapes=[pltpu.SemaphoreType.DMA((8 * len(steps),))],
        input_output_aliases={1 + len(got): 0} if rest else {},
    )(row, *got, *rest)


def local(pseudo_grad, kept_index, usage, module_params, momentum):
    forward, inverse = dct_tables()
    smem = pl.BlockSpec(memory_space=pltpu.SMEM)
    vmem = pl.BlockSpec(memory_space=pltpu.VMEM)
    z, half, q = lax.axis_index("z"), lax.axis_index("half"), lax.axis_index("quad")
    level = 2 * z + half
    used = lax.dynamic_slice_in_dim(usage, level, 1, 1).reshape(PATHS)
    used = jnp.concatenate([used, jnp.full((8,), q, jnp.int32)])
    row = lax.dynamic_slice_in_dim(usage, 32 * z, 32, 0).reshape(32, DEPTH, 2)
    row = lax.dynamic_index_in_dim(row, half, 2, keepdims=False).T.reshape(PATHS)
    place = jnp.where(jnp.arange(8) == 0, z, half * QUAD + q).astype(jnp.int32)
    row = jnp.concatenate([row, place])

    bases = call(
        base_kernel,
        [shaped((MINE * ROWS, COLS), F32)] * QUAD,
        in_specs=[smem, vmem, vmem],
        out_specs=[vmem] * QUAD,
    )(jnp.full((1,), q, jnp.int32), module_params, momentum)
    bases = [bases[0]] + [swap(bases[k], k) for k in range(1, QUAD)]

    anywhere = pl.BlockSpec(memory_space=pl.ANY)
    outgoing = call(
        pick_kernel,
        shaped((LEVELS, QUAD, SENT, 128), BF16),
        in_specs=[anywhere] * 3,
        out_specs=anywhere,
        scratch_shapes=[
            pltpu.VMEM((MINE, LEVELS, ROWS, WIDTH), BF16),
            pltpu.VMEM((MINE, LEVELS, 16, KEEP), jnp.int32),
            pltpu.VMEM((2, COLS, COLS), BF16),
            pltpu.VMEM((QUAD, MINE * LEVELS * ROWS, COLS), F32),
            pltpu.VMEM((2, LEVELS * QUAD, 128), jnp.int32),
            pltpu.VMEM((LEVELS, QUAD, SENT, 128), BF16),
            pltpu.SemaphoreType.DMA((2 + MINE + QUAD,)),
        ],
        limit=STREAM_LIMIT,
    )(pseudo_grad, kept_index, forward)
    got = lax.all_to_all(outgoing.reshape(DEVICES, SENT, 128), PATH, 0, 0, tiled=True)
    got, bases, row = lax.optimization_barrier((got, bases, row))

    average, squares, *pieces = call(
        sum_kernel,
        [shaped((QUAD, MINE * ROWS, COLS), BF16), shaped((16, 1, 128), F32)]
        + [shaped((MINE * ROWS, COLS), BF16)] * 3,
        in_specs=[smem, vmem],
        out_specs=[vmem] * 5,
        scratch_shapes=[pltpu.VMEM((8, DEVICES, 128), jnp.int32)]
        + [pltpu.VMEM((OPTIONS * ROWS, COLS), F32)] * 4
        + [pltpu.SMEM((OPTIONS,), jnp.int32)],
    )(used, got)
    squares = lax.all_to_all(squares, SQUARE_GROUP, 0, 0, tiled=True)

    fresh = call(
        fresh_kernel,
        shaped((OPTIONS * ROWS, COLS), BF16),
        in_specs=[smem] + [vmem] * 7,
        out_specs=vmem,
        scratch_shapes=[pltpu.VMEM((OPTIONS, 128), F32)],
    )(used, average, squares, inverse, *bases)
    before, after = [fresh], [fresh]
    for _ in range(2):
        before.append(along(before[-1], 1))
        after.append(along(after[-1], -1))
    pieces, _ = lax.optimization_barrier((pieces, fresh))
    pieces = [swap(piece, k + 1) for k, piece in enumerate(pieces)]
    packed = pack_all(NEAR[:3], row, [fresh, before[1], after[1]], 0, [])
    packed, pieces = lax.optimization_barrier((packed, pieces))
    packed = pack_all(NEAR[3:], row, [before[2], after[2]], 3, [packed])
    before2, after2 = before[2], after[2]
    near = lax.all_to_all(packed, ROW, 0, 0, tiled=True)
    before3, after3 = along(before2, 1), along(after2, -1)
    far = exchange_row(pack_row(FAR, row, [before3, after3, along(before3, 1)]))

    new_params, new_momentum = call(
        owner_kernel,
        [shaped((MINE, ROWS, WIDTH), BF16), shaped((MINE, ROWS, WIDTH), F32)],
        in_specs=[smem] + [vmem] * 8,
        out_specs=[vmem] * 2,
        scratch_shapes=[pltpu.VMEM((OPTIONS, 128), F32)],
    )(used, average, squares, inverse, module_params, momentum, *pieces)

    path_params = place_row(place_all_kernel, NEAR, row, [near], [])
    path_params = place_row(place_kernel, FAR, row, far, [path_params])
    return (new_params, new_momentum, path_params)


def solution(mesh):
    mesh = Mesh(mesh.devices.reshape(DEPTH, 2, QUAD, 4), PATH + ("shard",))
    return jax.shard_map(
        local,
        mesh=mesh,
        in_specs=(
            P(PATH, None, "shard", None),
            P(PATH, None, None, None),
            P(),
            P(PATH, "shard", None),
            P(PATH, "shard", None),
        ),
        out_specs=(
            P(PATH, "shard", None),
            P(PATH, "shard", None),
            P(PATH, None, "shard", None),
        ),
        check_vma=False,
    )
```

```python
import functools
import math

import jax
import jax.numpy as jnp
import ml_dtypes
import numpy as np
from jax import lax
from jax.experimental import pallas as pl
from jax.experimental.pallas import tpu as pltpu
from jax.sharding import Mesh
from jax.sharding import PartitionSpec as P

CH = 64
KEEP = 16
LEVELS = 16
OPTIONS = 16
ROWS = 16
WIDTH = 1024
PATHS = 256
DEVICES = 64
MINE = 4
QUAD = 4
COLS = WIDTH // QUAD
SENT = 40
F32 = jnp.float32
BF16 = jnp.bfloat16
CHUNKS = 4
VMEM_LIMIT = 40 * 1024 * 1024
STREAM_LIMIT = 56 * 1024 * 1024
PATH = ("z", "half", "quad")
ROW = ("half", "quad")
DEPTH = 8
ORDER = (0, 1, 4, 5, 2, 3, 6, 7)
NEAR = (0, -1, 1, -2, 2)
FAR = (-3, 3, 4)
SQUARE_GROUP = ("quad", "shard")


def dct_tables():
    k = np.arange(CH)[:, None]
    n = np.arange(CH)[None, :]
    scale = np.where(k == 0, math.sqrt(1.0 / CH), math.sqrt(2.0 / CH))
    table = np.kron(np.eye(4), scale * np.cos(math.pi * (2.0 * n + 1.0) * k / (2.0 * CH)))
    high = table.astype(ml_dtypes.bfloat16)
    low = (table - high.astype(np.float64)).astype(ml_dtypes.bfloat16)
    inverse = np.stack([high, low])
    return np.ascontiguousarray(inverse.transpose(0, 2, 1)), inverse


def dot2(values, table_ref):
    return jnp.dot(values, table_ref[0], preferred_element_type=F32) + jnp.dot(
        values, table_ref[1], preferred_element_type=F32
    )


def take_lanes(values, index):
    return jnp.take_along_axis(values, index, axis=1, mode="promise_in_bounds")


def lanes(rows):
    return lax.broadcasted_iota(jnp.int32, (rows, 128), 1)


def base_kernel(q_ref, params_ref, momentum_ref, *out_refs):
    for k in range(QUAD):
        at = pl.ds(pl.multiple_of((q_ref[0] ^ k) * COLS, COLS), COLS)
        for i in range(MINE):
            base = params_ref[i, :, at].astype(F32) - 0.567 * momentum_ref[i, :, at]
            out_refs[k][i * ROWS : (i + 1) * ROWS, :] = base


def sort_groups(values):
    lane = lanes(values.shape[0])
    size = 2
    while size <= KEEP:
        distance = size // 2
        while distance >= 1:
            other = take_lanes(values, lane ^ distance)
            upward = (lane & size) == 0 if size < KEEP else lane >= 0
            first = (lane & distance) == 0
            keep_least = first == upward
            values = jnp.where(keep_least, jnp.minimum(values, other), jnp.maximum(values, other))
            distance //= 2
        size *= 2
    return values


def gather_kept(kept_ref, pair):
    rows = LEVELS * 16
    repeat = (lanes(KEEP) % KEEP == lax.broadcasted_iota(jnp.int32, (KEEP, 128), 0)).astype(BF16)
    block = lax.broadcasted_iota(jnp.int32, (rows, 128), 0) % 4
    lane = lanes(rows)
    total = jnp.zeros((rows, 128), F32)
    for half in range(2):
        kept = kept_ref[pair * 2 + half].reshape(rows, KEEP).astype(F32).astype(BF16)
        spread = jnp.dot(kept, repeat, preferred_element_type=F32)
        total = jnp.where(lane // KEEP == half * 4 + block, spread, total)
    row = lax.broadcasted_iota(jnp.int32, (LEVELS * QUAD, rows), 0)
    column = lax.broadcasted_iota(jnp.int32, (LEVELS * QUAD, rows), 1)
    fold = (column // 4 == row).astype(BF16)
    return jnp.dot(fold, total.astype(BF16), preferred_element_type=F32).astype(jnp.int32)


def pick_kernel(
    grad_any,
    kept_any,
    table_any,
    out_any,
    grad_ref,
    kept_ref,
    table_ref,
    spectrum_ref,
    sorted_ref,
    out_ref,
    sems,
):
    kept = pltpu.make_async_copy(kept_any, kept_ref, sems.at[0])
    table = pltpu.make_async_copy(table_any, table_ref, sems.at[1])
    grads = [
        pltpu.make_async_copy(grad_any.at[p], grad_ref.at[p], sems.at[2 + p]) for p in range(MINE)
    ]
    emits = [
        pltpu.make_async_copy(out_ref.at[:, q], out_any.at[:, q], sems.at[2 + MINE + q])
        for q in range(QUAD)
    ]
    for copy in [kept, table] + grads:
        copy.start()
    kept.wait()
    for pair in range(2):
        sorted_ref[pair] = sort_groups(gather_kept(kept_ref, pair))
    lane = lanes(ROWS)
    shift = ((lane // KEEP) % 2) * CH
    for copy in [table] + grads:
        copy.wait()

    for q in range(QUAD):
        grad = grad_ref[:, :, :, q * COLS : (q + 1) * COLS].reshape(MINE * LEVELS * ROWS, COLS)
        spectrum_ref[q] = dot2(grad, table_ref)

        def pick(level, carry):
            for pair in range(2):
                row = sorted_ref[pair, pl.ds(level * QUAD + q, 1), :]
                index = jnp.broadcast_to(row, (ROWS, 128)) + shift

                def part(half, tile):
                    start = ((pair * 2 + half) * LEVELS + level) * ROWS
                    rows = pl.ds(pl.multiple_of(start, ROWS), ROWS)
                    return take_lanes(spectrum_ref[q, rows, tile * 128 : (tile + 1) * 128], index)

                first = jnp.where(lane < 32, part(0, 0), part(0, 1))
                second = jnp.where(lane < 96, part(1, 0), part(1, 1))
                picked = jnp.where(lane < 64, first, second)
                out_ref[level, q, pair * ROWS : (pair + 1) * ROWS, :] = picked.astype(BF16)
            rows = [sorted_ref[i, pl.ds(level * QUAD + q, 1), :].astype(F32) for i in range(2)]
            rows = jnp.concatenate(rows + [jnp.zeros((6, 128), F32)], axis=0)
            out_ref[level, q, 32:40, :] = rows.astype(BF16)
            return carry

        lax.fori_loop(0, LEVELS, pick, 0, unroll=True)
        emits[q].start()
    for copy in emits:
        copy.wait()


def sum_kernel(usage_ref, got_ref, avg_ref, square_ref, *rest):
    peer_refs = rest[:3]
    where_ref = rest[3]
    total_refs = rest[4:8]
    count_ref = rest[8]
    lane = lanes(8)
    block = lane // CH
    k = lane % CH
    for total in total_refs:
        total[...] = jnp.zeros_like(total)
    for o in range(OPTIONS):
        count_ref[o] = 0

    def invert(group, carry):
        at = pl.ds(pl.multiple_of(group * 8, 8), 8)
        index = got_ref[at, 32:40, :].astype(F32)
        for pair in range(2):
            rows = index[:, pair, :].astype(jnp.int32)
            for half in range(2):
                for tile in range(2):
                    place = half * 64 + (tile * 2 + block) * KEEP
                    held = take_lanes(rows, place)
                    for step in (8, 4, 2, 1):
                        probe = take_lanes(rows, place + step)
                        below = probe <= k
                        place = jnp.where(below, place + step, place)
                        held = jnp.where(below, probe, held)
                    found = jnp.where(held == k, place, -1)
                    where_ref[pair * 4 + half * 2 + tile, at, :] = found
        return carry

    lax.fori_loop(0, DEVICES // 8, invert, 0, unroll=4)

    def add(s, carry):
        for pair in range(2):
            values = got_ref[s, pair * ROWS : (pair + 1) * ROWS, :].astype(F32)
            for half in range(2):
                o = usage_ref[s * MINE + pair * 2 + half]
                count_ref[o] += 1
                rows = pl.ds(pl.multiple_of(o * ROWS, ROWS), ROWS)
                total = total_refs[pair * 2 + half]
                for tile in range(2):
                    index = jnp.broadcast_to(
                        where_ref[pair * 4 + half * 2 + tile, pl.ds(s, 1), :], (ROWS, 128)
                    )
                    spread = jnp.where(index >= 0, take_lanes(values, jnp.maximum(index, 0)), 0.0)
                    total[rows, tile * 128 : (tile + 1) * 128] += spread
        return carry

    lax.fori_loop(0, DEVICES, add, 0, unroll=32)

    squares = []
    for o in range(OPTIONS):
        at = slice(o * ROWS, (o + 1) * ROWS)
        summed = (total_refs[0][at, :] + total_refs[1][at, :]) + (
            total_refs[2][at, :] + total_refs[3][at, :]
        )
        average = summed / jnp.maximum(count_ref[o], 1).astype(F32)
        avg_ref[o // MINE, (o % MINE) * ROWS : (o % MINE + 1) * ROWS, :] = average.astype(BF16)
        square = average * average
        squares.append(jnp.sum(square[:, :128] + square[:, 128:], axis=0, keepdims=True))
    squares = jnp.sum(jnp.concatenate(squares, axis=0), axis=1, keepdims=True)
    diagonal = lax.broadcasted_iota(jnp.int32, (OPTIONS, 128), 0) == lanes(OPTIONS)
    squares = jnp.sum(jnp.where(diagonal, squares, 0.0), axis=0, keepdims=True)
    square_ref[...] = jnp.broadcast_to(squares[None], square_ref.shape)
    for i, peer_ref in enumerate(peer_refs):
        peer_ref[...] = avg_ref[usage_ref[PATHS] ^ (i + 1)]


def clip_factor(square_ref):
    total = jnp.sum(square_ref[...], axis=0)
    entries = 4.0 * ROWS * WIDTH
    factors = jnp.minimum(1.0, 0.3 / jnp.sqrt(total / entries + 1e-06))
    diagonal = lax.broadcasted_iota(jnp.int32, (OPTIONS, 128), 0) == lanes(OPTIONS)
    factors = jnp.sum(jnp.where(diagonal, factors, 0.0), axis=1, keepdims=True)
    return jnp.broadcast_to(factors, (OPTIONS, 128))


def fresh_kernel(usage_ref, avg_ref, square_ref, table_ref, *rest):
    base_refs = rest[:4]
    fresh_ref, factor_ref = rest[4:]
    factor_ref[...] = clip_factor(square_ref)
    for k in range(QUAD):
        owner = usage_ref[PATHS] ^ k
        delta = dot2(avg_ref[owner], table_ref)
        for i in range(MINE):
            module = owner * MINE + i
            at = slice(i * ROWS, (i + 1) * ROWS)
            change = (1.33 * factor_ref[pl.ds(module, 1), 0:1]) * delta[at, :]
            fresh = (base_refs[k][at, :] - change).astype(BF16)
            fresh_ref[pl.ds(pl.multiple_of(module * ROWS, ROWS), ROWS), :] = fresh


def neighbour(own, shift):
    chip = ((own >> 1) + (shift >> 1)) & 3
    return chip * 2 + ((own & 1) ^ (shift & 1))


def pack_kernel(steps, row_ref, *rest):
    block_refs, out_refs = rest[: len(steps)], rest[len(steps) :]
    for out_ref, shift in zip(out_refs, ORDER):
        target = neighbour(row_ref[PATHS + 1], shift)
        for b, step in enumerate(steps):
            origin = (row_ref[PATHS] + (step + DEPTH)) % DEPTH
            for p in range(MINE):
                o = row_ref[origin * 32 + target * MINE + p]
                rows = pl.ds(pl.multiple_of(o * ROWS, ROWS), ROWS)
                out_ref[b, p] = block_refs[b][rows, :]


def pack_all_kernel(steps, first, row_ref, *rest):
    block_refs = rest[: len(steps)]
    out_any, out_ref, sems = rest[-3:]
    copies = []
    for b, step in enumerate(steps):
        origin = (row_ref[PATHS] + (step + DEPTH)) % DEPTH
        for target in range(8):
            for p in range(MINE):
                o = row_ref[origin * 32 + target * MINE + p]
                rows = pl.ds(pl.multiple_of(o * ROWS, ROWS), ROWS)
                out_ref[target, b, p] = block_refs[b][rows, :]
        copies.append(pltpu.make_async_copy(out_ref.at[:, b], out_any.at[:, first + b], sems.at[b]))
        copies[-1].start()
    for copy in copies:
        copy.wait()


def owner_kernel(usage_ref, avg_ref, square_ref, table_ref, params_ref, momentum_ref, *rest):
    peer_refs = rest[:3]
    new_params_ref, new_momentum_ref, factor_ref = rest[3:]
    q = usage_ref[PATHS]
    factor_ref[...] = clip_factor(square_ref)
    for k in range(QUAD):
        at = pl.ds(pl.multiple_of((q ^ k) * COLS, COLS), COLS)
        average = avg_ref[q] if k == 0 else peer_refs[k - 1][...]
        delta = dot2(average, table_ref)
        for i in range(MINE):
            factor = factor_ref[pl.ds(q * MINE + i, 1), 0:1]
            clipped = delta[i * ROWS : (i + 1) * ROWS, :] * factor
            momentum = 0.9 * momentum_ref[i, :, at] + clipped
            new_momentum_ref[i, :, at] = momentum
            new = params_ref[i, :, at].astype(F32) - 0.7 * (clipped + 0.9 * momentum)
            new_params_ref[i, :, at] = new.astype(BF16)


def place_kernel(shifts, steps, row_ref, *rest):
    got_refs = rest[: len(shifts)]
    out_ref, sems = rest[-2:]
    copies = []
    for got_ref, shift in zip(got_refs, shifts):
        source = neighbour(row_ref[PATHS + 1], 8 - (shift & 6) + (shift & 1))
        columns = pl.ds(pl.multiple_of((source & 3) * COLS, COLS), COLS)
        for b, step in enumerate(steps):
            origin = (row_ref[PATHS] + (step + DEPTH)) % DEPTH
            level = origin * 2 + (source >> 2)
            copies.append(
                pltpu.make_async_copy(
                    got_ref.at[b], out_ref.at[:, level, :, columns], sems.at[len(copies)]
                )
            )
    for copy in copies:
        copy.start()
    for copy in copies:
        copy.wait()


def place_all_kernel(steps, row_ref, got_ref, *rest):
    out_ref, sems = rest[-2:]
    copies = []
    for b, step in enumerate(steps):
        origin = (row_ref[PATHS] + (step + DEPTH)) % DEPTH
        for half in range(2):
            for q in range(QUAD):
                copies.append(
                    pltpu.make_async_copy(
                        got_ref.at[half * QUAD + q, b],
                        out_ref.at[:, origin * 2 + half, :, pl.ds(q * COLS, COLS)],
                        sems.at[len(copies)],
                    )
                )
    for copy in copies:
        copy.start()
    for copy in copies:
        copy.wait()


def call(kernel, out_shape, limit=VMEM_LIMIT, **kwargs):
    return pl.pallas_call(
        kernel,
        out_shape=out_shape,
        compiler_params=pltpu.CompilerParams(vmem_limit_bytes=limit),
        **kwargs,
    )


def shaped(shape, dtype):
    return jax.ShapeDtypeStruct(shape, dtype)


def swap(values, k):
    return lax.ppermute(values, "quad", [(i, i ^ k) for i in range(QUAD)])


def along(values, k):
    return lax.ppermute(values, "z", [(i, (i + k) % DEPTH) for i in range(DEPTH)])


def pack_all(steps, row, blocks, first, rest):
    shape = (8, len(steps), MINE, ROWS, COLS)
    return call(
        functools.partial(pack_all_kernel, steps, first),
        shaped((8, len(NEAR), MINE, ROWS, COLS), BF16),
        in_specs=[pl.BlockSpec(memory_space=pltpu.SMEM)]
        + [pl.BlockSpec(memory_space=pltpu.VMEM)] * len(steps)
        + [pl.BlockSpec(memory_space=pltpu.HBM)] * len(rest),
        out_specs=pl.BlockSpec(memory_space=pltpu.HBM),
        scratch_shapes=[pltpu.VMEM(shape, BF16), pltpu.SemaphoreType.DMA((len(steps),))],
        input_output_aliases={1 + len(steps): 0} if rest else {},
    )(row, *blocks, *rest)


def pack_row(steps, row, blocks):
    vmem = pl.BlockSpec(memory_space=pltpu.VMEM)
    return call(
        functools.partial(pack_kernel, steps),
        [shaped((len(steps), MINE, ROWS, COLS), BF16)] * 8,
        in_specs=[pl.BlockSpec(memory_space=pltpu.SMEM)] + [vmem] * len(steps),
        out_specs=[vmem] * 8,
    )(row, *blocks)


def exchange_row(packed):
    got = [packed[0]]
    for values, shift in zip(packed[1:], ORDER[1:]):
        pairs = [(i, neighbour(i, shift)) for i in range(8)]
        got.append(lax.ppermute(values, ROW, pairs))
    return got


def place_row(kernel, steps, row, got, rest):
    anywhere = pl.BlockSpec(memory_space=pl.ANY)
    return call(
        functools.partial(kernel, steps),
        shaped((MINE, LEVELS, ROWS, WIDTH), BF16),
        in_specs=[pl.BlockSpec(memory_space=pltpu.SMEM)] + [anywhere] * len(got + rest),
        out_specs=anywhere,
        scratch_shapes=[pltpu.SemaphoreType.DMA((8 * len(steps),))],
        input_output_aliases={1 + len(got): 0} if rest else {},
    )(row, *got, *rest)


def local(pseudo_grad, kept_index, usage, module_params, momentum):
    forward, inverse = dct_tables()
    smem = pl.BlockSpec(memory_space=pltpu.SMEM)
    vmem = pl.BlockSpec(memory_space=pltpu.VMEM)
    z, half, q = lax.axis_index("z"), lax.axis_index("half"), lax.axis_index("quad")
    level = 2 * z + half
    used = lax.dynamic_slice_in_dim(usage, level, 1, 1).reshape(PATHS)
    used = jnp.concatenate([used, jnp.full((8,), q, jnp.int32)])
    row = lax.dynamic_slice_in_dim(usage, 32 * z, 32, 0).reshape(32, DEPTH, 2)
    row = lax.dynamic_index_in_dim(row, half, 2, keepdims=False).T.reshape(PATHS)
    place = jnp.where(jnp.arange(8) == 0, z, half * QUAD + q).astype(jnp.int32)
    row = jnp.concatenate([row, place])

    bases = call(
        base_kernel,
        [shaped((MINE * ROWS, COLS), F32)] * QUAD,
        in_specs=[smem, vmem, vmem],
        out_specs=[vmem] * QUAD,
    )(jnp.full((1,), q, jnp.int32), module_params, momentum)
    bases = [bases[0]] + [swap(bases[k], k) for k in range(1, QUAD)]

    anywhere = pl.BlockSpec(memory_space=pl.ANY)
    outgoing = call(
        pick_kernel,
        shaped((LEVELS, QUAD, SENT, 128), BF16),
        in_specs=[anywhere] * 3,
        out_specs=anywhere,
        scratch_shapes=[
            pltpu.VMEM((MINE, LEVELS, ROWS, WIDTH), BF16),
            pltpu.VMEM((MINE, LEVELS, 16, KEEP), jnp.int32),
            pltpu.VMEM((2, COLS, COLS), BF16),
            pltpu.VMEM((QUAD, MINE * LEVELS * ROWS, COLS), F32),
            pltpu.VMEM((2, LEVELS * QUAD, 128), jnp.int32),
            pltpu.VMEM((LEVELS, QUAD, SENT, 128), BF16),
            pltpu.SemaphoreType.DMA((2 + MINE + QUAD,)),
        ],
        limit=STREAM_LIMIT,
    )(pseudo_grad, kept_index, forward)
    got = lax.all_to_all(outgoing.reshape(DEVICES, SENT, 128), PATH, 0, 0, tiled=True)
    got, bases, row = lax.optimization_barrier((got, bases, row))

    average, squares, *pieces = call(
        sum_kernel,
        [shaped((QUAD, MINE * ROWS, COLS), BF16), shaped((16, 1, 128), F32)]
        + [shaped((MINE * ROWS, COLS), BF16)] * 3,
        in_specs=[smem, vmem],
        out_specs=[vmem] * 5,
        scratch_shapes=[pltpu.VMEM((8, DEVICES, 128), jnp.int32)]
        + [pltpu.VMEM((OPTIONS * ROWS, COLS), F32)] * 4
        + [pltpu.SMEM((OPTIONS,), jnp.int32)],
    )(used, got)
    squares = lax.all_to_all(squares, SQUARE_GROUP, 0, 0, tiled=True)

    fresh = call(
        fresh_kernel,
        shaped((OPTIONS * ROWS, COLS), BF16),
        in_specs=[smem] + [vmem] * 7,
        out_specs=vmem,
        scratch_shapes=[pltpu.VMEM((OPTIONS, 128), F32)],
    )(used, average, squares, inverse, *bases)
    before, after = [fresh], [fresh]
    for _ in range(2):
        before.append(along(before[-1], 1))
        after.append(along(after[-1], -1))
    pieces, _ = lax.optimization_barrier((pieces, fresh))
    pieces = [swap(piece, k + 1) for k, piece in enumerate(pieces)]
    packed = pack_all(NEAR[:3], row, [fresh, before[1], after[1]], 0, [])
    packed, pieces = lax.optimization_barrier((packed, pieces))
    packed = pack_all(NEAR[3:], row, [before[2], after[2]], 3, [packed])
    before2, after2 = before[2], after[2]
    near = lax.all_to_all(packed, ROW, 0, 0, tiled=True)
    before3, after3 = along(before2, 1), along(after2, -1)
    new_params, new_momentum = call(
        owner_kernel,
        [shaped((MINE, ROWS, WIDTH), BF16), shaped((MINE, ROWS, WIDTH), F32)],
        in_specs=[smem] + [vmem] * 8,
        out_specs=[vmem] * 2,
        scratch_shapes=[pltpu.VMEM((OPTIONS, 128), F32)],
    )(used, average, squares, inverse, module_params, momentum, *pieces)
    packed = pack_row(FAR, row, [before3, after3, along(before3, 1)])
    packed, new_params, new_momentum = lax.optimization_barrier((packed, new_params, new_momentum))
    far = exchange_row(packed)

    path_params = place_row(place_all_kernel, NEAR, row, [near], [])
    path_params = place_row(functools.partial(place_kernel, ORDER), FAR, row, far, [path_params])
    return (new_params, new_momentum, path_params)


def solution(mesh):
    mesh = Mesh(mesh.devices.reshape(DEPTH, 2, QUAD, 4), PATH + ("shard",))
    return jax.shard_map(
        local,
        mesh=mesh,
        in_specs=(
            P(PATH, None, "shard", None),
            P(PATH, None, None, None),
            P(),
            P(PATH, "shard", None),
            P(PATH, "shard", None),
        ),
        out_specs=(
            P(PATH, "shard", None),
            P(PATH, "shard", None),
            P(PATH, None, "shard", None),
        ),
        check_vma=False,
    )
```
